256 devices in a mesh: seq: 32 (over y, x, core), exp: 8 (over z).
Axes of the slice: x: 4, y: 4, z: 8, core: 2. Of those that a mesh axis runs over, the one named last changes fastest.
Arguments:
- queries: bfloat16 [4096, 2048], P('seq', 'exp'), may hold values from -10 to 10
- key_rows: bfloat16 [4096, 2048], P('seq', 'exp'), may hold values from -10 to 10
- value_rows: bfloat16 [4096, 2048], P('seq', 'exp'), may hold values from -6 to 6
- residual: bfloat16 [4096, 2048], P('seq'), may hold values from -20 to 20
- out_weight: bfloat16 [2048, 2048], P('exp'), may hold values from -1 to 1
- norm_gain: float32 [2048], replicated, may hold values from 0.5 to 1.5
- gate_weight: bfloat16 [64, 2048, 1408], P('seq', None, 'exp'), may hold values from -0.125 to 0.125
- up_weight: bfloat16 [64, 2048, 1408], P('seq', None, 'exp'), may hold values from -0.125 to 0.125
- down_weight: bfloat16 [64, 1408, 2048], P('seq', 'exp'), may hold values from -0.15625 to 0.15625
- routes: int32 [4096, 6], P('seq'), may hold values from 0 to 63, all different within a row; in each aligned block of 128 rows (0 to 127, 128 to 255, ...) at most 24 rows name the same one
- route_gates: float32 [4096, 6], P('seq'), may hold values from 0.2 to 1
- block_picks: int32 [8, 3], replicated, may hold values from 0 to 7, as said below
Outputs:
- layer_out: bfloat16 [4096, 2048], P(('seq', 'exp'))
The draws below stay inside these ranges and needn't reach their ends.
Inputs may be any that keep to these rules, and one draw needn't show every extreme that they name: `block_picks`: row b names block b first, then blocks at or before b, repeats allowed. `routes`: in each aligned block of 128 rows no expert is named by more than 24 rows, a bound that some block reaches.
All inputs are finite; a program needn't handle non-finite values.
Results may differ from the reference program's by a relative error of at most 0.015.
Values may be sent and summed in bfloat16 or wider, within the bound.
A program may use at most 64 MiB of HBM per device.

```python
import math
import jax
import jax.numpy as jnp
import numpy as np
from jax import lax

D = 2048
H = 16
HD = 128
FF = 1408
TOPK = 6
BLK = 512
TOPB = 3
TOK_SEQ = 128
TOKENS = 4096
EXPERTS = 64
MOST = 24
N_SEQ = 32
N_EXP = 8


def attention_pair(key):
    base_key = jax.random.fold_in(key, 7)
    key_query, key_keys = jax.random.split(base_key, 2)
    row_width = H * HD
    query_draw = jnp.clip(jax.random.normal(key_query, (TOKENS, row_width), jnp.float32), -6.0, 6.0)
    key_draw = jnp.clip(jax.random.normal(key_keys, (TOKENS, row_width), jnp.float32), -6.0, 6.0)
    return (query_draw, key_draw)


def draw_queries(key, part):
    return attention_pair(key)[0].astype(jnp.bfloat16)


def draw_key_rows(key, part):
    return attention_pair(key)[1].astype(jnp.bfloat16)


def draw_residual(key, part):
    key_base = jax.random.fold_in(jax.random.fold_in(key, 11), 0)
    return jnp.clip(jax.random.normal(key_base, (TOKENS, D), jnp.float32), -6.0, 6.0).astype(jnp.bfloat16)


def draw_block_picks(key, part):
    nblocks = TOKENS // BLK
    own_block = jnp.arange(nblocks, dtype=jnp.int32)
    raw_draw = jax.random.randint(jax.random.fold_in(key, 13), (nblocks, TOPB - 1), 0, 1 << 20, dtype=jnp.int32)
    earlier = raw_draw % (own_block[:, None] + 1)
    return jnp.concatenate([own_block[:, None], earlier], axis=1).astype(jnp.int32)


def block_levels(key, extent, shards, low, largest):
    factor_of = 1.0
    for axis_at, shards_of in shards:
        steps = jax.random.uniform(jax.random.fold_in(jax.random.fold_in(key, 6), axis_at), (shards_of,), jnp.float32, low / len(shards), largest / len(shards))
        factor_of = factor_of * jnp.repeat(jnp.exp(steps), extent[axis_at] // shards_of).reshape((-1,) + (1,) * (len(extent) - 1 - axis_at))
    return factor_of


def shared_out(rng, own, number, rows, amount, top, most, lean):
    ranking = jax.random.permutation(rng, amount)
    packed, common = shares(amount, rows * top, most, lean, True), shares(amount, rows * top, most, lean, False)
    places = jnp.arange(amount)

    def named(sizes, offset_by):
        used = int((sizes > 0).sum())
        fixed = max(1, used // 4)
        passed = fixed + (places - fixed + offset_by * (used - fixed)) % max(1, amount - fixed)
        return jnp.zeros((amount,), jnp.int32).at[ranking[jnp.where(places < fixed, places, passed)]].set(jnp.asarray(sizes, jnp.int32))

    sizes = jnp.where(number % 4 == 0, named(packed, number // 4), named(common, number - number // 4 - 1))
    mixed = jax.random.permutation(jax.random.fold_in(own, 3), amount)
    donor, receiver = mixed[0:amount // 2 * 2:2], mixed[1:amount // 2 * 2:2]
    room = jnp.minimum(sizes[donor] - 1, most - sizes[receiver]) // 2
    room = jnp.where((donor == ranking[0]) | (receiver == ranking[0]) | (sizes[receiver] == 0), 0, jnp.maximum(room, 0))
    passed = jax.random.randint(jax.random.fold_in(own, 4), (amount // 2,), 0, 1 << 20) % (room + 1)
    sizes = sizes.at[donor].add(-passed).at[receiver].add(passed)
    labels = jnp.searchsorted(jnp.cumsum(sizes), jnp.arange(rows * top), side="right").astype(jnp.int32)
    listing = labels.reshape(top, rows).T
    listing = listing[jax.random.permutation(jax.random.fold_in(own, 1), rows)]
    offset_by = jax.random.randint(jax.random.fold_in(own, 2), (rows, 1), 0, top)
    return jnp.take_along_axis(listing, (jnp.arange(top)[None, :] + offset_by) % top, axis=1)


def shares(amount, total, reach, lean, full):
    portions = [(1 << 20) // math.isqrt(standing ** lean) + 1 for standing in range(1, amount + 1)]
    largest = reach if full else min(reach, max(-(-total // amount), total * portions[0] // sum(portions)))
    least = 1 if total - largest >= amount - 1 else 0
    given, surplus = [largest] + [least] * (amount - 1), total - largest - least * (amount - 1)
    while surplus > 0:
        movable = [i for i in range(1, amount) if given[i] < largest] or [i for i in range(1, amount) if given[i] < reach]
        pool, left = sum([portions[i] for i in movable]), surplus
        for i in movable:
            addition = min(reach - given[i], max(1, left * portions[i] // pool), surplus)
            given[i] = given[i] + addition
            surplus = surplus - addition
    return np.array(given)


def noise(key, extent, deviation, reach, shards=(), held_as=jnp.bfloat16):
    result = jax.random.normal(key, extent, jnp.float32) * deviation
    if len(shards) > 0:
        result = block_levels(key, extent, shards, -0.22, 0.18) * result
    return jnp.clip(result, min=-reach, max=reach).astype(held_as)


def setup_inputs(seed: int = 0) -> dict:
    key_list = jax.random.split(jax.random.key(seed), 13)
    queries = draw_queries(jax.random.fold_in(key_list[12], 71), 0)
    key_rows = draw_key_rows(jax.random.fold_in(key_list[12], 71), 0)
    value_rows = noise(key_list[2], (TOKENS, H * HD), 1.0, 6.0, ((0, 32), (1, 8)))
    residual = draw_residual(jax.random.fold_in(key_list[12], 71), 0)
    out_weight = noise(key_list[4], (H * HD, D), (H * HD // 64) ** -0.5, 1.0, ((0, 8),))
    norm_gain = jnp.clip(1.0 + 0.1 * jax.random.normal(key_list[5], (D,), jnp.float32), 0.5, 1.5)
    gate_weight = noise(key_list[6], (EXPERTS, D, FF), D ** -0.5, 0.125, ((0, 32), (2, 8)))
    up_weight = noise(key_list[7], (EXPERTS, D, FF), D ** -0.5, 0.125, ((0, 32), (2, 8)))
    down_weight = noise(key_list[8], (EXPERTS, FF, D), FF ** -0.5, 0.15625, ((0, 32), (1, 8)))
    routes_keys = jax.random.split(jax.random.fold_in(key_list[9], 1), TOKENS // TOK_SEQ)
    routes_turns = jax.random.permutation(jax.random.fold_in(key_list[9], 3), TOKENS // TOK_SEQ)
    routes = jax.vmap(lambda own, number: shared_out(jax.random.fold_in(key_list[9], 2), own, number, TOK_SEQ, EXPERTS, TOPK, MOST, 2))(routes_keys, routes_turns).reshape((TOKENS, TOPK))
    route_gates = jnp.clip(0.2 + 0.8 * jax.random.uniform(key_list[10], (TOKENS, TOPK), jnp.float32) ** block_levels(key_list[10], (TOKENS, TOPK), ((0, 32),), -0.2, 0.2), 0.2, 1.0)
    block_picks = draw_block_picks(jax.random.fold_in(key_list[12], 71), 0)
    return dict(queries=queries, key_rows=key_rows, value_rows=value_rows, residual=residual, out_weight=out_weight, norm_gain=norm_gain, gate_weight=gate_weight, up_weight=up_weight, down_weight=down_weight, routes=routes, route_gates=route_gates, block_picks=block_picks)


def reference(queries, key_rows, value_rows, residual, out_weight, norm_gain, gate_weight, up_weight, down_weight, routes, route_gates, block_picks):
    positions = jnp.arange(TOKENS, dtype=jnp.int32)
    nblocks = TOKENS // BLK
    block_of = positions // BLK
    chosen = jnp.any(block_picks[:, :, None] == jnp.arange(nblocks, dtype=jnp.int32)[None, None, :], axis=1)
    allowed = chosen[block_of][:, block_of] & (positions[None, :] <= positions[:, None])
    score_scale = 1.0 / math.sqrt(HD)

    def one_head(head_index):
        first_col = (head_index * HD).astype(jnp.int32)
        q_head = lax.dynamic_slice_in_dim(queries, first_col, HD, 1)
        k_head = lax.dynamic_slice_in_dim(key_rows, first_col, HD, 1)
        v_head = lax.dynamic_slice_in_dim(value_rows, first_col, HD, 1)
        scores = jnp.dot(q_head, k_head.T, preferred_element_type=jnp.float32) * score_scale
        peak = lax.optimization_barrier(jnp.max(jnp.where(allowed, scores, -1e+30), axis=1, keepdims=True))
        expo = jnp.where(allowed, jnp.exp(scores - peak), 0.0)
        totals = lax.optimization_barrier(jnp.sum(expo, axis=1, keepdims=True))
        weights = expo.astype(jnp.bfloat16)
        mixed_values = jnp.dot(weights, v_head, preferred_element_type=jnp.float32) / totals
        return mixed_values.astype(jnp.bfloat16)
    per_head = lax.map(one_head, jnp.arange(H, dtype=jnp.int32))
    attended = jnp.transpose(per_head, (1, 0, 2)).reshape(TOKENS, H * HD)
    projected = jnp.dot(attended, out_weight, preferred_element_type=jnp.float32)
    hidden_state = residual.astype(jnp.float32) + projected
    mean_square = lax.optimization_barrier(jnp.mean(hidden_state * hidden_state, axis=-1, keepdims=True))
    normed = (hidden_state * lax.rsqrt(mean_square + 1e-06) * norm_gain.astype(jnp.float32)).astype(jnp.bfloat16)
    flat_routes = routes.reshape(-1)
    flat_gates = route_gates.reshape(-1)
    capacity = N_SEQ * MOST
    slice_width = FF // N_EXP

    def add_expert(running, expert):
        expert_hits = flat_routes == expert
        picked = jnp.nonzero(expert_hits, size=capacity, fill_value=0)[0].astype(jnp.int32)
        hit_count = jnp.sum(expert_hits.astype(jnp.int32))
        live_slot = jnp.arange(capacity, dtype=jnp.int32) < hit_count
        token_ids = (picked // TOPK).astype(jnp.int32)
        token_rows = normed[token_ids]
        gate_part = jnp.dot(token_rows, gate_weight[expert], preferred_element_type=jnp.float32)
        up_part = jnp.dot(token_rows, up_weight[expert], preferred_element_type=jnp.float32)
        inner_act = (jax.nn.silu(gate_part) * up_part).astype(jnp.bfloat16)
        pieces = jnp.einsum('csf,sfd->scd', inner_act.reshape(capacity, N_EXP, slice_width).astype(jnp.float32), down_weight[expert].reshape(N_EXP, slice_width, D).astype(jnp.float32))
        rounded = lax.optimization_barrier(pieces.astype(jnp.bfloat16))
        partial_value = lax.optimization_barrier(jnp.sum(rounded.astype(jnp.float32), axis=0))
        gate_values = jnp.where(live_slot, flat_gates[picked], 0.0)
        return (running.at[token_ids].add(partial_value * gate_values[:, None]), None)
    mixture, _ = lax.scan(add_expert, jnp.zeros((TOKENS, D), jnp.float32), jnp.arange(EXPERTS, dtype=jnp.int32))
    return (hidden_state + mixture).astype(jnp.bfloat16)
```

```python
import functools

import jax
import jax.numpy as jnp
from jax import lax
from jax.experimental import pallas as pl
from jax.experimental.pallas import tpu as pltpu
from jax.sharding import PartitionSpec as P

HD = 128
TOPK = 6
BLK = 512
INFO = 32
MESH = pl.DeviceIdType.MESH
F32 = jnp.float32
BF16 = jnp.bfloat16


def ring_offset(step):
    return step // 2 + (step % 2) * (3 - 2 * (step // 2))


class Gather:
    def __init__(self, place, half, pos, send_sem, recv_sem):
        self.place, self.half, self.pos = place, half, pos
        self.ss, self.rs = send_sem, recv_sem
        self.sent = []

    def send(self, ref, idx, dev):
        copy = pltpu.make_async_remote_copy(
            src_ref=ref,
            dst_ref=ref,
            send_sem=self.ss.at[idx],
            recv_sem=self.rs.at[idx],
            device_id={"seq": dev},
            device_id_type=MESH,
        )
        copy.start()

    def wait(self, ref, idx):
        pltpu.make_async_remote_copy(
            src_ref=ref,
            dst_ref=ref,
            send_sem=self.ss.at[idx],
            recv_sem=self.rs.at[idx],
            device_id={"seq": self.pos["sib"]},
            device_id_type=MESH,
        ).wait_recv()

    def wait_sent(self, ref, idx):
        pltpu.make_async_remote_copy(
            src_ref=ref,
            dst_ref=ref,
            send_sem=self.ss.at[idx],
            recv_sem=self.rs.at[idx],
            device_id={"seq": self.pos["sib"]},
            device_id_type=MESH,
        ).wait_send()

    def own_ready(self):
        p = self.pos
        block = self.place(p["k"], p["b"][0], p["a"][0])
        self.send(block, 0, p["ap"])
        self.send(block, 1, p["am"])
        self.send(block, 4, p["bp"])
        self.send(block, 8, p["bm"])
        self.send(block, 20, p["sib"])

    def first_near(self, j):
        p = self.pos
        block = self.place(p["k"], p["b"][0], p["a"][j])
        self.wait(block, j - 1)
        self.send(self.half(block, j - 1), 1 + j, p["ap"] if j == 1 else p["am"])
        self.send(block, 4 + j, p["bp"])
        self.send(block, 8 + j, p["bm"])
        self.send(block, 20 + j, p["sib"])

    def first_far(self):
        p = self.pos
        block = self.place(p["k"], p["b"][0], p["a"][3])
        self.wait(self.half(block, 0), 2)
        self.wait(self.half(block, 1), 3)
        self.send(block, 7, p["bp"])
        self.send(block, 11, p["bm"])
        self.send(block, 23, p["sib"])

    def second_near(self, j):
        p = self.pos
        block = self.place(p["k"], p["b"][1], p["a"][j])
        self.wait(block, 4 + j)
        self.send(self.half(block, 0), 12 + j, p["bp"])
        self.send(block, 24 + j, p["sib"])
        block = self.place(p["k"], p["b"][2], p["a"][j])
        self.wait(block, 8 + j)
        self.send(self.half(block, 1), 16 + j, p["bm"])
        self.send(block, 28 + j, p["sib"])

    def second_far(self, j):
        p = self.pos
        block = self.place(p["k"], p["b"][3], p["a"][j])
        self.wait(self.half(block, 0), 12 + j)
        self.wait(self.half(block, 1), 16 + j)
        self.send(block, 32 + j, p["sib"])

    def sibling(self, group):
        p = self.pos
        for j in range(4):
            block = self.place(1 - p["k"], p["a"][group], p["b"][j])
            self.wait(block, 20 + 4 * group + j)

    def before(self, step, other):
        if other:

            @pl.when(step == 0)
            def _():
                self.second_near(0)
                self.sibling(0)

            @pl.when(step == 1)
            def _():
                self.second_near(2)
                self.second_near(3)
                self.sibling(1)

            @pl.when(step == 2)
            def _():
                self.sibling(2)

            @pl.when(step == 3)
            def _():
                for j in range(4):
                    self.second_far(j)
                self.sibling(3)

        else:

            @pl.when(step == 0)
            def _():
                self.second_near(1)

    def drain(self):
        p = self.pos
        block = self.place(p["k"], p["b"][0], p["a"][0])
        for idx in range(36):
            part = self.half(block, 0) if idx in (2, 3) or 12 <= idx < 20 else block
            self.wait_sent(part, idx)


def add_rows(dst, srcs, rows, step):
    def body(i, carry):
        at = pl.ds(pl.multiple_of(i * step, step), step)
        total = dst[at, :].astype(F32)
        for src in srcs:
            total = total + src[at, :].astype(F32)
        dst[at, :] = total.astype(dst.dtype)
        return carry

    lax.fori_loop(0, rows // step, body, 0)


def ring_reduce(piece, low, high, near, far, ring, up, down, ss, rs, base, step):
    def copy(src, dst, idx, dev):
        return pltpu.make_async_remote_copy(
            src_ref=src,
            dst_ref=dst,
            send_sem=ss.at[base + idx],
            recv_sem=rs.at[base + idx],
            device_id={"seq": dev},
            device_id_type=MESH,
        )

    own, before, after, opposite = [piece(i) for i in ring]
    rows = own.shape[0]
    copies = [
        copy(low(opposite), far.at[0], 0, up),
        copy(high(opposite), far.at[1], 1, down),
        copy(high(after), high(near.at[0]), 2, up),
        copy(low(before), low(near.at[1]), 3, down),
    ]
    for c in copies:
        c.start()
    copies[0].wait_recv()
    add_rows(low(after), [far.at[0]], rows // 2, step)
    copies.append(copy(low(after), low(near.at[0]), 4, up))
    copies[4].start()
    copies[1].wait_recv()
    add_rows(high(before), [far.at[1]], rows // 2, step)
    copies.append(copy(high(before), high(near.at[1]), 5, down))
    copies[5].start()
    for c in copies[2:]:
        c.wait_recv()
    add_rows(own, [near.at[0], near.at[1]], rows, step)
    return copies


def kernel(
    nz,
    q_ref,
    k_ref,
    v_ref,
    info_ref,
    gain_ref,
    picks_ref,
    res_ref,
    wo_hbm,
    wg_hbm,
    wu_hbm,
    wd_hbm,
    out_ref,
    kv,
    tok,
    sib,
    near1,
    far1,
    near2,
    far2,
    zout,
    zin,
    zin2,
    pf,
    res,
    wo,
    wg,
    wu,
    wd,
    inner,
    gcol,
    mx,
    sm,
    acc,
    load_sem,
    kv_ss,
    kv_rs,
    tok_ss,
    tok_rs,
    sib_ss,
    sib_rs,
    red_ss,
    red_rs,
    z_ss,
    z_rs,
):
    T, D = q_ref.shape[0], wo.shape[1]
    NH = q_ref.shape[1] // HD
    R = T // nz
    me = lax.axis_index("seq")
    z = lax.axis_index("exp")
    k = me % 2
    x = (me // 2) % 4
    y = me // 8
    a0 = x * (1 - k) + y * k
    b0 = y * (1 - k) + x * k
    offs = (0, 3, 1, 2)
    a = [(a0 + o) % 4 for o in offs]
    b = [(b0 + o) % 4 for o in offs]

    def seq_of(first, second):
        return first * (2 + 6 * k) + second * (8 - 6 * k) + k

    pos = dict(
        k=k,
        a=a,
        b=b,
        ap=seq_of(a[2], b0),
        am=seq_of(a[1], b0),
        bp=seq_of(a0, b[2]),
        bm=seq_of(a0, b[1]),
        sib=me + 1 - 2 * k,
    )

    loads = [
        pltpu.make_async_copy(src, dst, load_sem.at[i])
        for i, (src, dst) in enumerate(
            (
                (wo_hbm, wo),
                (res_ref.at[pl.ds(pl.multiple_of(z * R, R), R)], res),
                (wg_hbm, wg),
                (wu_hbm, wu),
                (wd_hbm, wd),
            )
        )
    ]
    for load in loads:
        load.start()

    barrier = pltpu.get_barrier_semaphore()
    for name in ("ap", "am", "bp", "bm", "sib"):
        pl.semaphore_signal(barrier, inc=1, device_id={"seq": pos[name]}, device_id_type=MESH)
    for d in range(1, nz):
        pl.semaphore_signal(barrier, inc=1, device_id={"exp": (z + d) % nz}, device_id_type=MESH)

    own_kv = kv.at[k * 4 + b0, a0]
    own_kv[0:T, :] = k_ref[...]
    own_kv[T : 2 * T, :] = v_ref[...]
    own_kv[2 * T : 2 * T + INFO, :] = info_ref[...]
    mx[...] = jnp.full(mx.shape, -1e30, F32)
    sm[...] = jnp.zeros(sm.shape, F32)
    acc[...] = jnp.zeros(acc.shape, F32)
    pl.semaphore_wait(barrier, 4 + nz)

    kv_half = kv.shape[2] // 2
    kv_gather = Gather(
        lambda kk, g, i: kv.at[kk * 4 + g, i],
        lambda block, h: block.at[pl.ds(h * kv_half, kv_half)],
        pos,
        kv_ss,
        kv_rs,
    )
    kv_gather.own_ready()
    kv_gather.first_near(1)
    kv_gather.first_near(2)
    kv_gather.first_far()

    per_block = BLK // 128
    mine = me // per_block
    picks = [picks_ref[mine, i] for i in range(picks_ref.shape[1])]
    scale = HD ** (-0.5)

    def attend(kk, g):
        row = kk * 4 + g
        col = lax.broadcasted_iota(jnp.int32, (1, 4 * T), 1)
        seq_key = (col // T) * (2 + 6 * kk) + (g * (8 - 6 * kk) + kk)
        key_block = seq_key // per_block
        named = key_block == picks[0]
        for pick in picks[1:]:
            named = named | (key_block == pick)
        key_pos = jnp.where(named, seq_key * T + col % T, jnp.int32(1 << 30))
        query_pos = me * T + lax.broadcasted_iota(jnp.int32, (T, 1), 0)
        allowed = key_pos <= query_pos
        for h in range(NH):
            cols = slice(h * HD, (h + 1) * HD)
            keys = kv[row, :, 0:T, cols].reshape(4 * T, HD)
            values = kv[row, :, T : 2 * T, cols].reshape(4 * T, HD)
            s = (
                lax.dot_general(
                    q_ref[:, cols], keys, (((1,), (1,)), ((), ())), preferred_element_type=F32
                )
                * scale
            )
            s = jnp.where(allowed, s, -1e30)
            old = mx[h]
            new = jnp.maximum(old, jnp.max(s, axis=1, keepdims=True))
            w = jnp.where(allowed, jnp.exp(s - new[:, 0:1]), 0.0)
            fade = jnp.exp(old - new)
            mx[h] = new
            sm[h] = sm[h] * fade + jnp.sum(w, axis=1, keepdims=True)
            acc[h] = acc[h] * fade + jnp.dot(w.astype(BF16), values, preferred_element_type=F32)

    def attend_step(i, carry):
        off = ring_offset(i)
        kv_gather.before(i, True)
        attend(1 - k, (a0 + off) % 4)
        kv_gather.before(i, False)
        attend(k, (b0 + off) % 4)
        return carry

    lax.fori_loop(0, 4, attend_step, 0)

    loads[0].wait()
    for h in range(NH):
        head = (acc[h] / sm[h]).astype(BF16)
        term = jnp.dot(head, wo[h * HD : (h + 1) * HD, :], preferred_element_type=F32)
        pf[...] = term if h == 0 else pf[...] + term
    zout[...] = pf[...].astype(BF16)

    def z_copies(src_of, dst_of, base):
        copies = []
        for d in range(1, nz):
            there = (z + d) % nz
            copies.append(
                pltpu.make_async_remote_copy(
                    src_ref=src_of(there),
                    dst_ref=dst_of(d),
                    send_sem=z_ss.at[base + d - 1],
                    recv_sem=z_rs.at[base + d - 1],
                    device_id={"exp": there},
                    device_id_type=MESH,
                )
            )
        return copies

    def rows_of(there):
        return pl.ds(pl.multiple_of(there * R, R), R)

    sums = z_copies(lambda there: zout.at[rows_of(there)], lambda d: zin.at[d - 1], 0)
    for c in sums:
        c.start()
    loads[1].wait()
    hidden = res[...].astype(F32) + pf[rows_of(z), :]
    for d, c in enumerate(sums):
        c.wait_recv()
        hidden = hidden + zin[d].astype(F32)
    mean_square = jnp.mean(hidden * hidden, axis=-1, keepdims=True)
    normed = (hidden * lax.rsqrt(mean_square + 1e-06) * gain_ref[...]).astype(BF16)
    out_hidden = pf.at[0:R]
    for c in sums:
        c.wait_send()
    out_hidden[...] = hidden

    own_group = k * 4 + b0
    own_rows = tok.at[own_group, pl.ds(pl.multiple_of(a0 * T + z * R, R), R)]
    own_rows[...] = normed
    spread = z_copies(lambda there: own_rows, lambda d: own_rows, nz - 1)
    for c in spread:
        c.start()
    for d in range(1, nz):
        there = (z + nz - d) % nz
        landed = tok.at[own_group, pl.ds(pl.multiple_of(a0 * T + there * R, R), R)]
        pltpu.make_async_remote_copy(
            src_ref=landed,
            dst_ref=landed,
            send_sem=z_ss.at[nz - 2 + d],
            recv_sem=z_rs.at[nz - 2 + d],
            device_id={"exp": there},
            device_id_type=MESH,
        ).wait_recv()

    tok_gather = Gather(
        lambda kk, g, i: tok.at[kk * 4 + g, pl.ds(pl.multiple_of(i * T, T), T)],
        lambda block, h: block.at[pl.ds(h * (T // 2), T // 2)],
        pos,
        tok_ss,
        tok_rs,
    )
    tok_gather.own_ready()
    for load in loads[2:]:
        load.wait()
    tok_gather.first_near(1)
    tok_gather.first_near(2)
    tok_gather.first_far()

    tile = min(512, D)

    def experts(kk, g, store):
        row = kk * 4 + g
        for i in range(4):
            facts = kv[row, i, 2 * T : 2 * T + INFO, 0:T].astype(F32)
            named, gates = facts[0:8], facts[8:16] + facts[16:24]
            lane = lax.broadcasted_iota(jnp.int32, (128, T), 0)
            table = jnp.zeros((128, T), F32)
            for e in range(2):
                hit = named == (2 * me + e).astype(F32)
                gate = jnp.sum(jnp.where(hit, gates, 0.0), axis=0, keepdims=True)
                table = jnp.where(lane == e, gate, table)
            gcol[i * T : (i + 1) * T, :] = table.T
        for e in range(2):
            gate_part = jnp.dot(tok[row], wg[e], preferred_element_type=F32)
            up_part = jnp.dot(tok[row], wu[e], preferred_element_type=F32)
            act = gate_part / (1.0 + jnp.exp(-gate_part)) * up_part * gcol[:, e : e + 1]
            inner[e] = act.astype(BF16)
        for c in range(D // tile):
            cols = slice(c * tile, (c + 1) * tile)
            total = jnp.dot(inner[0], wd[0, :, cols], preferred_element_type=F32) + jnp.dot(
                inner[1], wd[1, :, cols], preferred_element_type=F32
            )
            store(row, g, cols, total)

    def hand_over(g, kk):
        return pltpu.make_async_remote_copy(
            src_ref=tok.at[kk * 4 + g],
            dst_ref=sib.at[g],
            send_sem=sib_ss.at[g],
            recv_sem=sib_rs.at[g],
            device_id={"seq": pos["sib"]},
            device_id_type=MESH,
        )

    def store_other(row, g, cols, total):
        tok[row, :, cols] = total.astype(BF16)

    def store_own(row, g, cols, total):
        sib[g, :, cols] = (total + sib[g, :, cols].astype(F32)).astype(BF16)

    def expert_step(i, carry):
        off = ring_offset(i)
        tok_gather.before(i, True)
        g = (a0 + off) % 4
        experts(1 - k, g, store_other)
        hand_over(g, 1 - k).start()
        tok_gather.before(i, False)
        g = (b0 + off) % 4
        hand_over(g, k).wait_recv()
        experts(k, g, store_own)
        return carry

    lax.fori_loop(0, 4, expert_step, 0)

    step = min(64, T // 2)
    first = ring_reduce(
        lambda i: sib.at[i],
        lambda r: r.at[0 : 2 * T],
        lambda r: r.at[2 * T : 4 * T],
        near1,
        far1,
        b,
        pos["bp"],
        pos["bm"],
        red_ss,
        red_rs,
        0,
        step,
    )
    own = sib.at[b0]
    second = ring_reduce(
        lambda i: own.at[pl.ds(pl.multiple_of(i * T, T), T)],
        lambda r: r.at[0 : T // 2],
        lambda r: r.at[T // 2 : T],
        near2,
        far2,
        a,
        pos["ap"],
        pos["am"],
        red_ss,
        red_rs,
        6,
        step,
    )
    block = own.at[pl.ds(pl.multiple_of(a0 * T, T), T)]
    last = z_copies(lambda there: block.at[rows_of(there)], lambda d: zin2.at[d - 1], 2 * (nz - 1))
    for c in last:
        c.start()
    total = pf[0:R, :] + block[rows_of(z), :].astype(F32)
    for d, c in enumerate(last):
        c.wait_recv()
        total = total + zin2[d].astype(F32)
    out_ref[...] = total.astype(BF16)

    for c in first + second + last + spread:
        c.wait_send()
    for g in range(4):
        hand_over(g, 1 - k).wait_send()
    kv_gather.drain()
    tok_gather.drain()


def per_device(
    queries,
    key_rows,
    value_rows,
    residual,
    out_weight,
    norm_gain,
    gate_weight,
    up_weight,
    down_weight,
    routes,
    route_gates,
    block_picks,
):
    nz = lax.axis_size("exp")
    T, D = residual.shape
    R = T // nz
    F = gate_weight.shape[2]
    cols = queries.shape[1]
    nh = cols // HD
    high = lax.reduce_precision(route_gates, 8, 7)
    low = route_gates - high
    facts = jnp.concatenate(
        [
            jnp.pad(routes.astype(F32).T, ((0, 2), (0, 0)), constant_values=-1.0),
            jnp.pad(high.T, ((0, 2), (0, 0))),
            jnp.pad(low.T, ((0, INFO - 22), (0, 0))),
        ],
        axis=0,
    )
    info = jnp.pad(facts, ((0, 0), (0, cols - T))).astype(BF16)
    vmem = pl.BlockSpec(memory_space=pltpu.VMEM)
    anywhere = pl.BlockSpec(memory_space=pl.ANY)
    dma = pltpu.SemaphoreType.DMA
    return pl.pallas_call(
        functools.partial(kernel, nz),
        out_shape=jax.ShapeDtypeStruct((R, D), BF16),
        in_specs=[vmem] * 5 + [pl.BlockSpec(memory_space=pltpu.SMEM)] + [anywhere] * 5,
        out_specs=vmem,
        scratch_shapes=[
            pltpu.VMEM((8, 4, 2 * T + INFO, cols), BF16),
            pltpu.VMEM((8, 4 * T, D), BF16),
            pltpu.VMEM((4, 4 * T, D), BF16),
            pltpu.VMEM((2, 4 * T, D), BF16),
            pltpu.VMEM((2, 2 * T, D), BF16),
            pltpu.VMEM((2, T, D), BF16),
            pltpu.VMEM((2, T // 2, D), BF16),
            pltpu.VMEM((T, D), BF16),
            pltpu.VMEM((nz - 1, R, D), BF16),
            pltpu.VMEM((nz - 1, R, D), BF16),
            pltpu.VMEM((T, D), F32),
            pltpu.VMEM((R, D), BF16),
            pltpu.VMEM(out_weight.shape, BF16),
            pltpu.VMEM(gate_weight.shape, BF16),
            pltpu.VMEM(up_weight.shape, BF16),
            pltpu.VMEM(down_weight.shape, BF16),
            pltpu.VMEM((2, 4 * T, F), BF16),
            pltpu.VMEM((4 * T, 128), F32),
            pltpu.VMEM((nh, T, 128), F32),
            pltpu.VMEM((nh, T, 128), F32),
            pltpu.VMEM((nh, T, HD), F32),
            dma((5,)),
            dma((36,)),
            dma((36,)),
            dma((36,)),
            dma((36,)),
            dma((4,)),
            dma((4,)),
            dma((12,)),
            dma((12,)),
            dma((3 * (nz - 1),)),
            dma((3 * (nz - 1),)),
        ],
        compiler_params=pltpu.CompilerParams(
            collective_id=0, has_side_effects=True, vmem_limit_bytes=60 * 1024 * 1024
        ),
        cost_estimate=pl.CostEstimate(flops=2 * 10**10, bytes_accessed=10**7, transcendentals=10**6),
    )(
        queries,
        key_rows,
        value_rows,
        info,
        norm_gain.reshape(1, D),
        block_picks,
        residual,
        out_weight,
        gate_weight,
        up_weight,
        down_weight,
    )


def solution(mesh):
    placed = (
        P("seq", "exp"),
        P("seq", "exp"),
        P("seq", "exp"),
        P("seq", None),
        P("exp", None),
        P(),
        P("seq", None, "exp"),
        P("seq", None, "exp"),
        P("seq", "exp", None),
        P("seq", None),
        P("seq", None),
        P(),
    )
    return jax.shard_map(
        per_device, mesh=mesh, in_specs=placed, out_specs=P(("seq", "exp"), None), check_vma=False
    )
```

```python
import functools

import jax
import jax.numpy as jnp
from jax import lax
from jax.experimental import pallas as pl
from jax.experimental.pallas import tpu as pltpu
from jax.sharding import PartitionSpec as P

HD = 128
TOPK = 6
BLK = 512
INFO = 32
MESH = pl.DeviceIdType.MESH
F32 = jnp.float32
BF16 = jnp.bfloat16


def ring_offset(step):
    return step // 2 + (step % 2) * (3 - 2 * (step // 2))


class Gather:
    def __init__(self, place, half, pos, send_sem, recv_sem, base=0):
        self.place, self.half, self.pos = place, half, pos
        self.ss, self.rs, self.base = send_sem, recv_sem, base

    def send(self, ref, idx, dev):
        copy = pltpu.make_async_remote_copy(
            src_ref=ref,
            dst_ref=ref,
            send_sem=self.ss.at[self.base + idx],
            recv_sem=self.rs.at[self.base + idx],
            device_id={"seq": dev},
            device_id_type=MESH,
        )
        copy.start()

    def wait(self, ref, idx):
        pltpu.make_async_remote_copy(
            src_ref=ref,
            dst_ref=ref,
            send_sem=self.ss.at[self.base + idx],
            recv_sem=self.rs.at[self.base + idx],
            device_id={"seq": self.pos["sib"]},
            device_id_type=MESH,
        ).wait_recv()

    def wait_sent(self, ref, idx):
        pltpu.make_async_remote_copy(
            src_ref=ref,
            dst_ref=ref,
            send_sem=self.ss.at[self.base + idx],
            recv_sem=self.rs.at[self.base + idx],
            device_id={"seq": self.pos["sib"]},
            device_id_type=MESH,
        ).wait_send()

    def own_ready(self):
        p = self.pos
        block = self.place(p["k"], p["b"][0], p["a"][0])
        self.send(block, 0, p["ap"])
        self.send(block, 1, p["am"])
        self.send(block, 4, p["bp"])
        self.send(block, 8, p["bm"])
        self.send(block, 20, p["sib"])

    def first_near(self, j):
        p = self.pos
        block = self.place(p["k"], p["b"][0], p["a"][j])
        self.wait(block, j - 1)
        self.send(self.half(block, j - 1), 1 + j, p["ap"] if j == 1 else p["am"])
        self.send(block, 4 + j, p["bp"])
        self.send(block, 8 + j, p["bm"])
        self.send(block, 20 + j, p["sib"])

    def first_far(self):
        p = self.pos
        block = self.place(p["k"], p["b"][0], p["a"][3])
        self.wait(self.half(block, 0), 2)
        self.wait(self.half(block, 1), 3)
        self.send(block, 7, p["bp"])
        self.send(block, 11, p["bm"])
        self.send(block, 23, p["sib"])

    def second_near(self, j):
        p = self.pos
        block = self.place(p["k"], p["b"][1], p["a"][j])
        self.wait(block, 4 + j)
        self.send(self.half(block, 0), 12 + j, p["bp"])
        self.send(block, 24 + j, p["sib"])
        block = self.place(p["k"], p["b"][2], p["a"][j])
        self.wait(block, 8 + j)
        self.send(self.half(block, 1), 16 + j, p["bm"])
        self.send(block, 28 + j, p["sib"])

    def second_far(self, j):
        p = self.pos
        block = self.place(p["k"], p["b"][3], p["a"][j])
        self.wait(self.half(block, 0), 12 + j)
        self.wait(self.half(block, 1), 16 + j)
        self.send(block, 32 + j, p["sib"])

    def sibling(self, group):
        p = self.pos
        for j in range(4):
            block = self.place(1 - p["k"], p["a"][group], p["b"][j])
            self.wait(block, 20 + 4 * group + j)

    def drain(self):
        p = self.pos
        block = self.place(p["k"], p["b"][0], p["a"][0])
        for idx in range(36):
            part = self.half(block, 0) if idx in (2, 3) or 12 <= idx < 20 else block
            self.wait_sent(part, idx)


def add_rows(dst, srcs, rows, step):
    def body(i, carry):
        at = pl.ds(pl.multiple_of(i * step, step), step)
        total = dst[at, :].astype(F32)
        for src in srcs:
            total = total + src[at, :].astype(F32)
        dst[at, :] = total.astype(dst.dtype)
        return carry

    lax.fori_loop(0, rows // step, body, 0)


class Scatter:
    def __init__(self, piece, half, near, far, ring, up, down, ss, rs, base, step):
        self.own, self.before, self.after, self.opposite = [piece(i) for i in ring]
        self.half, self.near, self.far = half, near, far
        self.up, self.down, self.step = up, down, step
        self.ss, self.rs, self.base = ss, rs, base
        self.copies = []

    def copy(self, src, dst, dev):
        at = self.base + len(self.copies)
        copy = pltpu.make_async_remote_copy(
            src_ref=src,
            dst_ref=dst,
            send_sem=self.ss.at[at],
            recv_sem=self.rs.at[at],
            device_id={"seq": dev},
            device_id_type=MESH,
        )
        self.copies.append(copy)

    def describe(self):
        half, near, far = self.half, self.near, self.far
        self.copy(half(self.opposite, 0), far.at[0], self.up)
        self.copy(half(self.opposite, 1), far.at[1], self.down)
        self.copy(half(self.after, 1), half(near.at[0], 1), self.up)
        self.copy(half(self.before, 0), half(near.at[1], 0), self.down)
        self.copy(half(self.after, 0), half(near.at[0], 0), self.up)
        self.copy(half(self.before, 1), half(near.at[1], 1), self.down)

    def start(self):
        for copy in self.copies[:4]:
            copy.start()

    def pass_on(self):
        rows = self.own.shape[0] // 2
        self.copies[0].wait_recv()
        add_rows(self.half(self.after, 0), [self.far.at[0]], rows, self.step)
        self.copies[4].start()
        self.copies[1].wait_recv()
        add_rows(self.half(self.before, 1), [self.far.at[1]], rows, self.step)
        self.copies[5].start()

    def finish(self):
        for copy in self.copies[2:]:
            copy.wait_recv()
        add_rows(self.own, [self.near.at[0], self.near.at[1]], self.own.shape[0], self.step)

    def drain(self):
        for copy in self.copies:
            copy.wait_send()


def kernel(
    nz,
    q_ref,
    k_ref,
    v_ref,
    routes_ref,
    gates_ref,
    gain_ref,
    picks_ref,
    res_hbm,
    wo_hbm,
    wg_hbm,
    wu_hbm,
    wd_hbm,
    out_ref,
    kv,
    tok,
    sib,
    near1,
    far1,
    near2,
    far2,
    zout,
    zin,
    zin2,
    pf,
    hid,
    facts,
    res,
    wo,
    wgu,
    wd,
    inner,
    table,
    gates,
    mx,
    sm,
    acc,
    load_sem,
    kv_ss,
    kv_rs,
    tok_ss,
    tok_rs,
    sib_ss,
    sib_rs,
    red_ss,
    red_rs,
    sum_ss,
    sum_rs,
    row_ss,
    row_rs,
    last_ss,
    last_rs,
):
    T, D = q_ref.shape[0], wo.shape[1]
    NH = q_ref.shape[1] // HD
    R = T // nz
    C = T // 2
    FF = wg_hbm.shape[1]
    WIDE = wd.shape[0]
    me = lax.axis_index("seq")
    z = lax.axis_index("exp")
    k = me % 2
    x = (me // 2) % 4
    y = me // 8
    a0 = x * (1 - k) + y * k
    b0 = y * (1 - k) + x * k
    offs = (0, 3, 1, 2)
    a = [(a0 + o) % 4 for o in offs]
    b = [(b0 + o) % 4 for o in offs]

    def seq_of(first, second):
        return first * (2 + 6 * k) + second * (8 - 6 * k) + k

    pos = dict(
        k=k,
        a=a,
        b=b,
        ap=seq_of(a[2], b0),
        am=seq_of(a[1], b0),
        bp=seq_of(a0, b[2]),
        bm=seq_of(a0, b[1]),
        sib=me + 1 - 2 * k,
    )

    barrier = pltpu.get_barrier_semaphore()
    for name in ("ap", "am", "bp", "bm", "sib"):
        pl.semaphore_signal(barrier, inc=1, device_id={"seq": pos[name]}, device_id_type=MESH)
    for d in range(1, nz):
        pl.semaphore_signal(barrier, inc=1, device_id={"exp": (z + d) % nz}, device_id_type=MESH)

    own_kv = kv.at[k * 4 + b0, a0]
    own_kv[0:T, :] = k_ref[...]
    own_kv[T : 2 * T, :] = v_ref[...]
    gate = gates_ref[...]
    high = gate.astype(BF16).astype(F32)
    facts[...] = jnp.zeros(facts.shape, F32)
    facts[0:8, :] = jnp.full((8, T), -1.0, F32)
    facts[0:TOPK, :] = routes_ref[...].astype(F32)
    facts[8 : 8 + TOPK, :] = high
    facts[16 : 16 + TOPK, :] = gate - high
    own_kv[2 * T : 2 * T + INFO, 0:T] = facts[...].astype(BF16)
    own_kv[2 * T : 2 * T + INFO, T:] = jnp.zeros((INFO, own_kv.shape[1] - T), BF16)
    pl.semaphore_wait(barrier, 4 + nz)

    kv_half = kv.shape[2] // 2
    kv_gather = Gather(
        lambda kk, g, i: kv.at[kk * 4 + g, i],
        lambda block, h: block.at[pl.ds(h * kv_half, kv_half)],
        pos,
        kv_ss,
        kv_rs,
    )
    kv_gather.own_ready()

    loads = [
        pltpu.make_async_copy(src, dst, load_sem.at[i])
        for i, (src, dst) in enumerate(
            [
                (wo_hbm, wo),
                (res_hbm.at[pl.ds(pl.multiple_of(z * R, R), R)], res),
            ]
            + [(wg_hbm.at[e], wgu.at[e * FF : (e + 1) * FF]) for e in range(2)]
            + [(wu_hbm.at[e], wgu.at[WIDE + e * FF : WIDE + (e + 1) * FF]) for e in range(2)]
            + [(wd_hbm.at[e], wd.at[e * FF : (e + 1) * FF]) for e in range(2)]
        )
    ]
    for load in loads:
        load.start()
    spare = jnp.zeros((WIDE - 2 * FF, D), BF16)
    wgu[2 * FF : WIDE, :] = spare
    wgu[WIDE + 2 * FF : 2 * WIDE, :] = spare
    wd[2 * FF : WIDE, :] = spare
    mx[...] = jnp.full(mx.shape, -1e30, F32)
    sm[...] = jnp.zeros(sm.shape, F32)
    acc[...] = jnp.zeros(acc.shape, F32)

    kv_gather.first_near(1)
    kv_gather.first_near(2)
    kv_gather.first_far()

    per_block = BLK // 128
    mine = me // per_block
    picks = [picks_ref[i, mine] for i in range(picks_ref.shape[0])]
    scale = HD ** (-0.5)

    def attend(kk, g):
        row = kk * 4 + g
        col = lax.broadcasted_iota(jnp.int32, (1, 4 * T), 1)
        seq_key = (col // T) * (2 + 6 * kk) + (g * (8 - 6 * kk) + kk)
        key_block = seq_key // per_block
        named = key_block == picks[0]
        for pick in picks[1:]:
            named = named | (key_block == pick)
        key_pos = jnp.where(named, seq_key * T + col % T, jnp.int32(1 << 30))
        query_pos = me * T + lax.broadcasted_iota(jnp.int32, (T, 1), 0)
        allowed = key_pos <= query_pos
        for h in range(NH):
            cols = slice(h * HD, (h + 1) * HD)
            keys = kv[row, :, 0:T, cols].reshape(4 * T, HD)
            values = kv[row, :, T : 2 * T, cols].reshape(4 * T, HD)
            s = (
                lax.dot_general(
                    q_ref[:, cols], keys, (((1,), (1,)), ((), ())), preferred_element_type=F32
                )
                * scale
            )
            s = jnp.where(allowed, s, -1e30)
            old = mx[h]
            new = jnp.maximum(old, jnp.max(s, axis=1, keepdims=True))
            w = jnp.where(allowed, jnp.exp(s - new[:, 0:1]), 0.0)
            fade = jnp.exp(old - new)
            mx[h] = new
            sm[h] = sm[h] * fade + jnp.sum(w, axis=1, keepdims=True)
            acc[h] = acc[h] * fade + jnp.dot(w.astype(BF16), values, preferred_element_type=F32)

    def attend_step(i, carry):
        @pl.when(i == 0)
        def _():
            kv_gather.second_near(0)
            kv_gather.second_near(1)
            kv_gather.sibling(0)

        @pl.when(i == 1)
        def _():
            kv_gather.second_near(2)
            kv_gather.second_near(3)
            kv_gather.sibling(1)

        @pl.when(i == 2)
        def _():
            kv_gather.sibling(2)

        @pl.when(i == 3)
        def _():
            for j in range(4):
                kv_gather.second_far(j)
            kv_gather.sibling(3)

        off = ring_offset(i)
        attend(1 - k, (a0 + off) % 4)
        attend(k, (b0 + off) % 4)
        return carry

    lax.fori_loop(0, 4, attend_step, 0)

    loads[0].wait()
    for h in range(NH):
        head = (acc[h] / sm[h]).astype(BF16)
        term = jnp.dot(head, wo[h * HD : (h + 1) * HD, :], preferred_element_type=F32)
        pf[...] = term if h == 0 else pf[...] + term
    zout[...] = pf[...].astype(BF16)

    def z_copy(src, dst, there, ss, rs):
        d = (there + nz - z) % nz
        return pltpu.make_async_remote_copy(
            src_ref=src,
            dst_ref=dst,
            send_sem=ss.at[d],
            recv_sem=rs.at[d],
            device_id={"exp": there},
            device_id_type=MESH,
        )

    def rows_of(there):
        return pl.ds(pl.multiple_of(there * R, R), R)

    order = list(range(0, nz, 2)) + list(range(1, nz, 2))

    def sum_copy(there):
        d = (there + nz - z) % nz
        return z_copy(zout.at[rows_of(there)], zin.at[d], there, sum_ss, sum_rs)

    for there in order:

        @pl.when(z != there)
        def _(there=there):
            sum_copy(there).start()

    def gate_step(row, carry):
        for i in range(4):
            told = kv[row, i, 2 * T : 2 * T + INFO, 0:T].astype(F32)
            named, given = told[0:8], told[8:16] + told[16:24]
            lane = lax.broadcasted_iota(jnp.int32, (128, T), 0)
            grid = jnp.zeros((128, T), F32)
            for e in range(2):
                hit = named == (2 * me + e).astype(F32)
                worth = jnp.sum(jnp.where(hit, given, 0.0), axis=0, keepdims=True)
                grid = jnp.where(lane == e, worth, grid)
            table[...] = grid.T
            for there in range(nz):
                at = i * C + (there // 2) * R
                gates[there % 2, row, at : at + R, :] = table[there * R : (there + 1) * R, :]
        return carry

    lax.fori_loop(0, 8, gate_step, 0)
    loads[1].wait()
    hidden = res[...].astype(F32) + pf[rows_of(z), :]
    for d in range(1, nz):
        z_copy(zin.at[d], zin.at[d], (z + d) % nz, sum_ss, sum_rs).wait_recv()
        hidden = hidden + zin[d].astype(F32)
    mean_square = jnp.mean(hidden * hidden, axis=-1, keepdims=True)
    hid[...] = hidden
    normed = (hidden * lax.rsqrt(mean_square + 1e-06) * gain_ref[...]).astype(BF16)

    own_group = k * 4 + b0

    def rows_at(there):
        return tok.at[
            there % 2, own_group, pl.ds(pl.multiple_of(a0 * C + (there // 2) * R, R), R)
        ]

    rows_at(z)[...] = normed

    def spread():
        for d in range(1, nz):
            z_copy(rows_at(z), rows_at(z), (z + d) % nz, row_ss, row_rs).start()

    def spread_arrived(parity):
        for there in range(parity, nz, 2):

            @pl.when(z != there)
            def _(there=there):
                back = (z + nz - there) % nz
                z_copy(rows_at(there), rows_at(there), (z + back) % nz, row_ss, row_rs).wait_recv()

    @pl.when(z % 2 == 0)
    def _():
        spread()

    spread_arrived(0)

    @pl.when(z % 2 == 1)
    def _():
        spread()

    def gather_of(c):
        return Gather(
            lambda kk, g, i: tok.at[c, kk * 4 + g, pl.ds(pl.multiple_of(i * C, C), C)],
            lambda block, h: block.at[pl.ds(h * (C // 2), C // 2)],
            pos,
            tok_ss,
            tok_rs,
            36 * c,
        )

    even, odd = gather_of(0), gather_of(1)
    even.own_ready()
    for load in loads[2:]:
        load.wait()
    even.first_near(1)
    even.first_near(2)
    even.first_far()
    spread_arrived(1)
    odd.own_ready()

    tile = min(512, D)

    def experts(c, kk, g, store):
        row = kk * 4 + g
        both = lax.dot_general(
            tok[c, row], wgu[...], (((1,), (1,)), ((), ())), preferred_element_type=F32
        )
        gate_part, up_part = both[:, 0:WIDE], both[:, WIDE : 2 * WIDE]
        lane = lax.broadcasted_iota(jnp.int32, (4 * C, WIDE), 1)
        worth = jnp.where(lane < FF, gates[c, row, :, 0:1], gates[c, row, :, 1:2])
        inner[...] = (gate_part / (1.0 + jnp.exp(-gate_part)) * up_part * worth).astype(BF16)
        for t in range(D // tile):
            cols = slice(t * tile, (t + 1) * tile)
            store(row, cols, jnp.dot(inner[...], wd[:, cols], preferred_element_type=F32))

    def hand_over(c, g, kk):
        return pltpu.make_async_remote_copy(
            src_ref=tok.at[c, kk * 4 + g],
            dst_ref=sib.at[c, g],
            send_sem=sib_ss.at[c * 4 + g],
            recv_sem=sib_rs.at[c * 4 + g],
            device_id={"seq": pos["sib"]},
            device_id_type=MESH,
        )

    step = min(64, C // 2)

    def scatters(c):
        first = Scatter(
            lambda i: sib.at[c, i],
            lambda r, h: r.at[pl.ds(h * 2 * C, 2 * C)],
            near1.at[c],
            far1.at[c],
            b,
            pos["bp"],
            pos["bm"],
            red_ss,
            red_rs,
            12 * c,
            step,
        )
        first.describe()
        second = Scatter(
            lambda i: sib.at[c, b0, pl.ds(pl.multiple_of(i * C, C), C)],
            lambda r, h: r.at[pl.ds(h * (C // 2), C // 2)],
            near2.at[c],
            far2.at[c],
            a,
            pos["ap"],
            pos["am"],
            red_ss,
            red_rs,
            12 * c + 6,
            step // 2,
        )
        second.describe()
        return first, second

    even_first, even_second = scatters(0)
    odd_first, odd_second = scatters(1)

    def expert_step(s, carry):
        c = s // 4
        off = ring_offset(s % 4)

        @pl.when(s == 0)
        def _():
            even.second_near(0)
            even.second_near(1)
            even.sibling(0)

        @pl.when(s == 1)
        def _():
            even.second_near(2)
            even.second_near(3)
            even.sibling(1)
            odd.first_near(1)
            odd.first_near(2)

        @pl.when(s == 2)
        def _():
            odd.first_far()
            even.sibling(2)

        @pl.when(s == 3)
        def _():
            for j in range(4):
                even.second_far(j)
            even.sibling(3)

        @pl.when(s == 4)
        def _():
            even_first.start()
            odd.second_near(0)
            odd.second_near(1)
            odd.sibling(0)

        @pl.when(s == 5)
        def _():
            odd.second_near(2)
            odd.second_near(3)
            odd.sibling(1)

        @pl.when(s == 6)
        def _():
            even_first.pass_on()
            odd.sibling(2)

        @pl.when(s == 7)
        def _():
            for j in range(4):
                odd.second_far(j)
            odd.sibling(3)

        g = (a0 + off) % 4

        def store_other(row, cols, total):
            tok[c, row, :, cols] = total.astype(BF16)

        experts(c, 1 - k, g, store_other)
        hand_over(c, g, 1 - k).start()
        g = (b0 + off) % 4
        hand_over(c, g, k).wait_recv()

        def store_own(row, cols, total, g=g):
            sib[c, g, :, cols] = (total + sib[c, g, :, cols].astype(F32)).astype(BF16)

        experts(c, k, g, store_own)
        return carry

    lax.fori_loop(0, 8, expert_step, 0)

    def last_rows(c, there):
        return sib.at[c, b0, pl.ds(pl.multiple_of(a0 * C + (there // 2) * R, R), R)]

    def last_copies(c, act):
        for there in range(c, nz, 2):

            @pl.when(z != there)
            def _(there=there):
                d = (there + nz - z) % nz
                act(z_copy(last_rows(c, there), zin2.at[d], there, last_ss, last_rs))

    odd_first.start()
    even_first.finish()
    even_second.start()
    odd_first.pass_on()
    even_second.pass_on()
    even_second.finish()
    last_copies(0, lambda copy: copy.start())
    odd_first.finish()
    odd_second.start()
    odd_second.pass_on()
    odd_second.finish()
    last_copies(1, lambda copy: copy.start())
    total = hid[...] + last_rows(z % 2, z)[...].astype(F32)
    for d in range(1, nz):
        z_copy(zin2.at[d], zin2.at[d], (z + d) % nz, last_ss, last_rs).wait_recv()
        total = total + zin2[d].astype(F32)
    out_ref[...] = total.astype(BF16)

    for scatter in (even_first, even_second, odd_first, odd_second):
        scatter.drain()
    for c in range(2):
        last_copies(c, lambda copy: copy.wait_send())
        for g in range(4):
            hand_over(c, g, 1 - k).wait_send()
    for there in order:

        @pl.when(z != there)
        def _(there=there):
            sum_copy(there).wait_send()

    for d in range(1, nz):
        z_copy(rows_at(z), rows_at(z), (z + d) % nz, row_ss, row_rs).wait_send()
    kv_gather.drain()
    even.drain()
    odd.drain()


def per_device(
    queries,
    key_rows,
    value_rows,
    residual,
    out_weight,
    norm_gain,
    gate_weight,
    up_weight,
    down_weight,
    routes,
    route_gates,
    block_picks,
):
    nz = lax.axis_size("exp")
    T, D = residual.shape
    R = T // nz
    C = T // 2
    F = gate_weight.shape[2]
    wide = -(-2 * F // 128) * 128
    cols = queries.shape[1]
    nh = cols // HD
    vmem = pl.BlockSpec(memory_space=pltpu.VMEM)
    anywhere = pl.BlockSpec(memory_space=pl.ANY)
    dma = pltpu.SemaphoreType.DMA
    return pl.pallas_call(
        functools.partial(kernel, nz),
        out_shape=jax.ShapeDtypeStruct((R, D), BF16),
        in_specs=[vmem] * 6 + [pl.BlockSpec(memory_space=pltpu.SMEM)] + [anywhere] * 5,
        out_specs=vmem,
        scratch_shapes=[
            pltpu.VMEM((8, 4, 2 * T + INFO, cols), BF16),
            pltpu.VMEM((2, 8, 4 * C, D), BF16),
            pltpu.VMEM((2, 4, 4 * C, D), BF16),
            pltpu.VMEM((2, 2, 4 * C, D), BF16),
            pltpu.VMEM((2, 2, 2 * C, D), BF16),
            pltpu.VMEM((2, 2, C, D), BF16),
            pltpu.VMEM((2, 2, C // 2, D), BF16),
            pltpu.VMEM((T, D), BF16),
            pltpu.VMEM((nz, R, D), BF16),
            pltpu.VMEM((nz, R, D), BF16),
            pltpu.VMEM((T, D), F32),
            pltpu.VMEM((R, D), F32),
            pltpu.VMEM((INFO, T), F32),
            pltpu.VMEM((R, D), BF16),
            pltpu.VMEM(out_weight.shape, BF16),
            pltpu.VMEM((2 * wide, D), BF16),
            pltpu.VMEM((wide, D), BF16),
            pltpu.VMEM((4 * C, wide), BF16),
            pltpu.VMEM((T, 128), F32),
            pltpu.VMEM((2, 8, 4 * C, 128), F32),
            pltpu.VMEM((nh, T, 128), F32),
            pltpu.VMEM((nh, T, 128), F32),
            pltpu.VMEM((nh, T, HD), F32),
            dma((8,)),
            dma((36,)),
            dma((36,)),
            dma((72,)),
            dma((72,)),
            dma((8,)),
            dma((8,)),
            dma((24,)),
            dma((24,)),
            dma((nz,)),
            dma((nz,)),
            dma((nz,)),
            dma((nz,)),
            dma((nz,)),
            dma((nz,)),
        ],
        compiler_params=pltpu.CompilerParams(
            collective_id=0, has_side_effects=True, vmem_limit_bytes=60 * 1024 * 1024
        ),
        cost_estimate=pl.CostEstimate(flops=2 * 10**10, bytes_accessed=10**7, transcendentals=10**6),
    )(
        queries,
        key_rows,
        value_rows,
        routes.T,
        route_gates.T,
        norm_gain.reshape(1, D),
        block_picks.T,
        residual,
        out_weight,
        jnp.swapaxes(gate_weight, 1, 2),
        jnp.swapaxes(up_weight, 1, 2),
        down_weight,
    )


def solution(mesh):
    placed = (
        P("seq", "exp"),
        P("seq", "exp"),
        P("seq", "exp"),
        P("seq", None),
        P("exp", None),
        P(),
        P("seq", None, "exp"),
        P("seq", None, "exp"),
        P("seq", "exp", None),
        P("seq", None),
        P("seq", None),
        P(),
    )
    return jax.shard_map(
        per_device, mesh=mesh, in_specs=placed, out_specs=P(("seq", "exp"), None), check_vma=False
    )
```

```python
import functools

import jax
import jax.numpy as jnp
from jax import lax
from jax.experimental import pallas as pl
from jax.experimental.pallas import tpu as pltpu
from jax.sharding import PartitionSpec as P

HD = 128
TOPK = 6
BLK = 512
INFO = 32
MESH = pl.DeviceIdType.MESH
F32 = jnp.float32
BF16 = jnp.bfloat16


def ring_offset(step):
    return step // 2 + (step % 2) * (3 - 2 * (step // 2))


class Gather:
    def __init__(self, place, half, pos, send_sem, recv_sem, base=0, direct=False):
        self.place, self.half, self.pos = place, half, pos
        self.ss, self.rs, self.base, self.direct = send_sem, recv_sem, base, direct

    def send(self, ref, idx, dev):
        copy = pltpu.make_async_remote_copy(
            src_ref=ref,
            dst_ref=ref,
            send_sem=self.ss.at[self.base + idx],
            recv_sem=self.rs.at[self.base + idx],
            device_id={"seq": dev},
            device_id_type=MESH,
        )
        copy.start()

    def wait(self, ref, idx):
        pltpu.make_async_remote_copy(
            src_ref=ref,
            dst_ref=ref,
            send_sem=self.ss.at[self.base + idx],
            recv_sem=self.rs.at[self.base + idx],
            device_id={"seq": self.pos["sib"]},
            device_id_type=MESH,
        ).wait_recv()

    def wait_sent(self, ref, idx):
        pltpu.make_async_remote_copy(
            src_ref=ref,
            dst_ref=ref,
            send_sem=self.ss.at[self.base + idx],
            recv_sem=self.rs.at[self.base + idx],
            device_id={"seq": self.pos["sib"]},
            device_id_type=MESH,
        ).wait_send()

    def own_ready(self):
        p = self.pos
        block = self.place(p["k"], p["b"][0], p["a"][0])
        self.send(block, 0, p["ap"])
        self.send(block, 1, p["am"])
        if self.direct:
            self.send(block, 2, p["aa"])
        self.send(block, 4, p["bp"])
        self.send(block, 8, p["bm"])
        self.send(block, 20, p["sib"])

    def first_near(self, j):
        p = self.pos
        block = self.place(p["k"], p["b"][0], p["a"][j])
        self.wait(block, j - 1)
        if not self.direct:
            self.send(self.half(block, j - 1), 1 + j, p["ap"] if j == 1 else p["am"])
        self.send(block, 4 + j, p["bp"])
        self.send(block, 8 + j, p["bm"])
        self.send(block, 20 + j, p["sib"])

    def first_far(self):
        p = self.pos
        block = self.place(p["k"], p["b"][0], p["a"][3])
        if self.direct:
            self.wait(block, 2)
        else:
            self.wait(self.half(block, 0), 2)
            self.wait(self.half(block, 1), 3)
        self.send(block, 7, p["bp"])
        self.send(block, 11, p["bm"])
        self.send(block, 23, p["sib"])

    def second_near(self, j):
        p = self.pos
        block = self.place(p["k"], p["b"][1], p["a"][j])
        self.wait(block, 4 + j)
        self.send(self.half(block, 0), 12 + j, p["bp"])
        self.send(block, 24 + j, p["sib"])
        block = self.place(p["k"], p["b"][2], p["a"][j])
        self.wait(block, 8 + j)
        self.send(self.half(block, 1), 16 + j, p["bm"])
        self.send(block, 28 + j, p["sib"])

    def second_far(self, j):
        p = self.pos
        block = self.place(p["k"], p["b"][3], p["a"][j])
        self.wait(self.half(block, 0), 12 + j)
        self.wait(self.half(block, 1), 16 + j)
        self.send(block, 32 + j, p["sib"])

    def sibling(self, group):
        p = self.pos
        for j in range(4):
            block = self.place(1 - p["k"], p["a"][group], p["b"][j])
            self.wait(block, 20 + 4 * group + j)

    def drain(self):
        p = self.pos
        block = self.place(p["k"], p["b"][0], p["a"][0])
        for idx in range(36):
            if self.direct and idx == 3:
                continue
            halved = 12 <= idx < 20 or (idx in (2, 3) and not self.direct)
            part = self.half(block, 0) if halved else block
            self.wait_sent(part, idx)


def add_rows(dst, srcs, rows, step):
    def body(i, carry):
        at = pl.ds(pl.multiple_of(i * step, step), step)
        total = dst[at, :].astype(F32)
        for src in srcs:
            total = total + src[at, :].astype(F32)
        dst[at, :] = total.astype(dst.dtype)
        return carry

    lax.fori_loop(0, rows // step, body, 0)


class Scatter:
    def __init__(self, piece, half, near, far, ring, up, down, ss, rs, base, step):
        self.own, self.before, self.after, self.opposite = [piece(i) for i in ring]
        self.half, self.near, self.far = half, near, far
        self.up, self.down, self.step = up, down, step
        self.ss, self.rs, self.base = ss, rs, base
        self.copies = []

    def copy(self, src, dst, dev):
        at = self.base + len(self.copies)
        copy = pltpu.make_async_remote_copy(
            src_ref=src,
            dst_ref=dst,
            send_sem=self.ss.at[at],
            recv_sem=self.rs.at[at],
            device_id={"seq": dev},
            device_id_type=MESH,
        )
        self.copies.append(copy)

    def describe(self):
        half, near, far = self.half, self.near, self.far
        self.copy(half(self.opposite, 0), far.at[0], self.up)
        self.copy(half(self.opposite, 1), far.at[1], self.down)
        self.copy(half(self.after, 1), half(near.at[0], 1), self.up)
        self.copy(half(self.before, 0), half(near.at[1], 0), self.down)
        self.copy(half(self.after, 0), half(near.at[0], 0), self.up)
        self.copy(half(self.before, 1), half(near.at[1], 1), self.down)

    def start(self):
        for copy in self.copies[:4]:
            copy.start()

    def pass_on(self):
        rows = self.own.shape[0] // 2
        self.copies[0].wait_recv()
        add_rows(self.half(self.after, 0), [self.far.at[0]], rows, self.step)
        self.copies[4].start()
        self.copies[1].wait_recv()
        add_rows(self.half(self.before, 1), [self.far.at[1]], rows, self.step)
        self.copies[5].start()

    def finish(self):
        for copy in self.copies[2:]:
            copy.wait_recv()
        add_rows(self.own, [self.near.at[0], self.near.at[1]], self.own.shape[0], self.step)

    def drain(self):
        for copy in self.copies:
            copy.wait_send()


def kernel(
    nz,
    q_ref,
    k_ref,
    v_ref,
    routes_ref,
    gates_ref,
    gain_ref,
    picks_ref,
    res_hbm,
    wo_hbm,
    wg_hbm,
    wu_hbm,
    wd_hbm,
    out_ref,
    kv,
    tok,
    sib,
    near1,
    far1,
    near2,
    far2,
    zout,
    zin,
    zin2,
    pf,
    hid,
    facts,
    res,
    wo,
    wgu,
    wd,
    inner,
    table,
    gates,
    mx,
    sm,
    acc,
    load_sem,
    kv_ss,
    kv_rs,
    tok_ss,
    tok_rs,
    sib_ss,
    sib_rs,
    red_ss,
    red_rs,
    sum_ss,
    sum_rs,
    row_ss,
    row_rs,
    last_ss,
    last_rs,
    told_sem,
):
    T, D = q_ref.shape[0], wo.shape[1]
    NH = q_ref.shape[1] // HD
    R = T // nz
    C = T // 2
    FF = wg_hbm.shape[1]
    WIDE = wd.shape[0]
    me = lax.axis_index("seq")
    z = lax.axis_index("exp")
    k = me % 2
    x = (me // 2) % 4
    y = me // 8
    a0 = x * (1 - k) + y * k
    b0 = y * (1 - k) + x * k
    offs = (0, 3, 1, 2)
    a = [(a0 + o) % 4 for o in offs]
    b = [(b0 + o) % 4 for o in offs]

    def seq_of(first, second):
        return first * (2 + 6 * k) + second * (8 - 6 * k) + k

    pos = dict(
        k=k,
        a=a,
        b=b,
        ap=seq_of(a[2], b0),
        am=seq_of(a[1], b0),
        aa=seq_of(a[3], b0),
        bp=seq_of(a0, b[2]),
        bm=seq_of(a0, b[1]),
        sib=me + 1 - 2 * k,
    )

    barrier = pltpu.get_barrier_semaphore()
    for name in ("ap", "am", "aa", "bp", "bm", "sib"):
        pl.semaphore_signal(barrier, inc=1, device_id={"seq": pos[name]}, device_id_type=MESH)
    around = ((z + 1) % nz, (z + nz - 1) % nz)
    for there in around:
        pl.semaphore_signal(barrier, inc=1, device_id={"exp": there}, device_id_type=MESH)

    own_kv = kv.at[k * 4 + b0, a0]
    own_kv[0:T, :] = k_ref[...]
    own_kv[T : 2 * T, :] = v_ref[...]
    gate = gates_ref[...]
    high = gate.astype(BF16).astype(F32)
    facts[...] = jnp.zeros(facts.shape, F32)
    facts[0:8, :] = jnp.full((8, T), -1.0, F32)
    facts[0:TOPK, :] = routes_ref[...].astype(F32)
    facts[8 : 8 + TOPK, :] = high
    facts[16 : 16 + TOPK, :] = gate - high
    own_kv[2 * T : 2 * T + INFO, 0:T] = facts[...].astype(BF16)
    own_kv[2 * T : 2 * T + INFO, T:] = jnp.zeros((INFO, own_kv.shape[1] - T), BF16)
    pl.semaphore_wait(barrier, 8)

    kv_half = kv.shape[2] // 2
    kv_gather = Gather(
        lambda kk, g, i: kv.at[kk * 4 + g, i],
        lambda block, h: block.at[pl.ds(h * kv_half, kv_half)],
        pos,
        kv_ss,
        kv_rs,
        direct=True,
    )
    kv_gather.own_ready()

    def tell(r):
        for there in around:
            pl.semaphore_signal(
                told_sem.at[r], inc=1, device_id={"exp": there}, device_id_type=MESH
            )

    def heard(r):
        pl.semaphore_wait(told_sem.at[r], 2)

    tell(0)
    loads = [
        pltpu.make_async_copy(src, dst, load_sem.at[i])
        for i, (src, dst) in enumerate(
            [
                (wo_hbm, wo),
                (res_hbm.at[pl.ds(pl.multiple_of(z * R, R), R)], res),
            ]
            + [(wg_hbm.at[e], wgu.at[e * FF : (e + 1) * FF]) for e in range(2)]
            + [(wu_hbm.at[e], wgu.at[WIDE + e * FF : WIDE + (e + 1) * FF]) for e in range(2)]
            + [(wd_hbm.at[e], wd.at[e * FF : (e + 1) * FF]) for e in range(2)]
        )
    ]
    for load in loads:
        load.start()
    spare = jnp.zeros((WIDE - 2 * FF, D), BF16)
    wgu[2 * FF : WIDE, :] = spare
    wgu[WIDE + 2 * FF : 2 * WIDE, :] = spare
    wd[2 * FF : WIDE, :] = spare
    mx[...] = jnp.full(mx.shape, -1e30, F32)
    sm[...] = jnp.zeros(sm.shape, F32)
    acc[...] = jnp.zeros(acc.shape, F32)

    kv_gather.first_near(1)
    kv_gather.first_near(2)
    heard(0)
    tell(1)
    kv_gather.first_far()
    heard(1)
    tell(2)

    per_block = BLK // 128
    mine = me // per_block
    picks = [picks_ref[i, mine] for i in range(picks_ref.shape[0])]
    scale = HD ** (-0.5)

    def attend(kk, g):
        row = kk * 4 + g
        col = lax.broadcasted_iota(jnp.int32, (1, 4 * T), 1)
        seq_key = (col // T) * (2 + 6 * kk) + (g * (8 - 6 * kk) + kk)
        key_block = seq_key // per_block
        named = key_block == picks[0]
        for pick in picks[1:]:
            named = named | (key_block == pick)
        key_pos = jnp.where(named, seq_key * T + col % T, jnp.int32(1 << 30))
        query_pos = me * T + lax.broadcasted_iota(jnp.int32, (T, 1), 0)
        allowed = key_pos <= query_pos
        for h in range(NH):
            cols = slice(h * HD, (h + 1) * HD)
            keys = kv[row, :, 0:T, cols].reshape(4 * T, HD)
            values = kv[row, :, T : 2 * T, cols].reshape(4 * T, HD)
            s = (
                lax.dot_general(
                    q_ref[:, cols], keys, (((1,), (1,)), ((), ())), preferred_element_type=F32
                )
                * scale
            )
            s = jnp.where(allowed, s, -1e30)
            old = mx[h]
            new = jnp.maximum(old, jnp.max(s, axis=1, keepdims=True))
            w = jnp.where(allowed, jnp.exp(s - new[:, 0:1]), 0.0)
            fade = jnp.exp(old - new)
            mx[h] = new
            sm[h] = sm[h] * fade + jnp.sum(w, axis=1, keepdims=True)
            acc[h] = acc[h] * fade + jnp.dot(w.astype(BF16), values, preferred_element_type=F32)

    def attend_step(i, carry):
        @pl.when(i == 0)
        def _():
            kv_gather.second_near(0)
            kv_gather.second_near(1)
            kv_gather.sibling(0)

        @pl.when(i == 1)
        def _():
            kv_gather.second_near(2)
            kv_gather.second_near(3)
            kv_gather.sibling(1)

        @pl.when(i == 2)
        def _():
            kv_gather.sibling(2)

        @pl.when(i == 3)
        def _():
            for j in range(4):
                kv_gather.second_far(j)
            kv_gather.sibling(3)

        off = ring_offset(i)
        attend(1 - k, (a0 + off) % 4)
        attend(k, (b0 + off) % 4)
        return carry

    lax.fori_loop(0, 4, attend_step, 0)

    loads[0].wait()
    for h in range(NH):
        head = (acc[h] / sm[h]).astype(BF16)
        term = jnp.dot(head, wo[h * HD : (h + 1) * HD, :], preferred_element_type=F32)
        pf[...] = term if h == 0 else pf[...] + term
    zout[...] = pf[...].astype(BF16)

    def z_copy(src, dst, there, ss, rs):
        d = (there + nz - z) % nz
        return pltpu.make_async_remote_copy(
            src_ref=src,
            dst_ref=dst,
            send_sem=ss.at[d],
            recv_sem=rs.at[d],
            device_id={"exp": there},
            device_id_type=MESH,
        )

    def rows_of(there):
        return pl.ds(pl.multiple_of(there * R, R), R)

    heard(2)
    order = list(range(0, nz, 2)) + list(range(1, nz, 2))

    def sum_copy(there):
        d = (there + nz - z) % nz
        return z_copy(zout.at[rows_of(there)], zin.at[d], there, sum_ss, sum_rs)

    for there in order:

        @pl.when(z != there)
        def _(there=there):
            sum_copy(there).start()

    def gate_step(row, carry):
        for i in range(4):
            told = kv[row, i, 2 * T : 2 * T + INFO, 0:T].astype(F32)
            named, given = told[0:8], told[8:16] + told[16:24]
            lane = lax.broadcasted_iota(jnp.int32, (128, T), 0)
            grid = jnp.zeros((128, T), F32)
            for e in range(2):
                hit = named == (2 * me + e).astype(F32)
                worth = jnp.sum(jnp.where(hit, given, 0.0), axis=0, keepdims=True)
                grid = jnp.where(lane == e, worth, grid)
            table[...] = grid.T
            for there in range(nz):
                at = i * C + (there // 2) * R
                gates[there % 2, row, at : at + R, :] = table[there * R : (there + 1) * R, :]
        return carry

    lax.fori_loop(0, 8, gate_step, 0)
    loads[1].wait()
    hidden = res[...].astype(F32) + pf[rows_of(z), :]
    for d in range(1, nz):
        z_copy(zin.at[d], zin.at[d], (z + d) % nz, sum_ss, sum_rs).wait_recv()
        hidden = hidden + zin[d].astype(F32)
    mean_square = jnp.mean(hidden * hidden, axis=-1, keepdims=True)
    hid[...] = hidden
    normed = (hidden * lax.rsqrt(mean_square + 1e-06) * gain_ref[...]).astype(BF16)

    own_group = k * 4 + b0

    def rows_at(there):
        return tok.at[
            there % 2, own_group, pl.ds(pl.multiple_of(a0 * C + (there // 2) * R, R), R)
        ]

    rows_at(z)[...] = normed

    def spread():
        for d in range(1, nz):
            z_copy(rows_at(z), rows_at(z), (z + d) % nz, row_ss, row_rs).start()

    def spread_arrived(parity):
        for there in range(parity, nz, 2):

            @pl.when(z != there)
            def _(there=there):
                back = (z + nz - there) % nz
                z_copy(rows_at(there), rows_at(there), (z + back) % nz, row_ss, row_rs).wait_recv()

    @pl.when(z % 2 == 0)
    def _():
        spread()

    spread_arrived(0)

    @pl.when(z % 2 == 1)
    def _():
        spread()

    def gather_of(c):
        return Gather(
            lambda kk, g, i: tok.at[c, kk * 4 + g, pl.ds(pl.multiple_of(i * C, C), C)],
            lambda block, h: block.at[pl.ds(h * (C // 2), C // 2)],
            pos,
            tok_ss,
            tok_rs,
            36 * c,
            direct=c == 0,
        )

    even, odd = gather_of(0), gather_of(1)
    even.own_ready()
    for load in loads[2:]:
        load.wait()
    even.first_near(1)
    even.first_near(2)
    even.first_far()
    spread_arrived(1)
    odd.own_ready()

    tile = min(512, D)

    def experts(c, kk, g, store, between):
        row = kk * 4 + g
        both = lax.dot_general(
            tok[c, row], wgu[...], (((1,), (1,)), ((), ())), preferred_element_type=F32
        )
        gate_part, up_part = both[:, 0:WIDE], both[:, WIDE : 2 * WIDE]
        lane = lax.broadcasted_iota(jnp.int32, (4 * C, WIDE), 1)
        worth = jnp.where(lane < FF, gates[c, row, :, 0:1], gates[c, row, :, 1:2])
        inner[...] = (gate_part / (1.0 + jnp.exp(-gate_part)) * up_part * worth).astype(BF16)
        between()
        for t in range(D // tile):
            cols = slice(t * tile, (t + 1) * tile)
            store(row, cols, jnp.dot(inner[...], wd[:, cols], preferred_element_type=F32))

    def hand_over(c, g, kk):
        return pltpu.make_async_remote_copy(
            src_ref=tok.at[c, kk * 4 + g],
            dst_ref=sib.at[c, g],
            send_sem=sib_ss.at[c * 4 + g],
            recv_sem=sib_rs.at[c * 4 + g],
            device_id={"seq": pos["sib"]},
            device_id_type=MESH,
        )

    step = min(64, C // 2)

    def scatters(c):
        first = Scatter(
            lambda i: sib.at[c, i],
            lambda r, h: r.at[pl.ds(h * 2 * C, 2 * C)],
            near1.at[c],
            far1.at[c],
            b,
            pos["bp"],
            pos["bm"],
            red_ss,
            red_rs,
            12 * c,
            step,
        )
        first.describe()
        second = Scatter(
            lambda i: sib.at[c, b0, pl.ds(pl.multiple_of(i * C, C), C)],
            lambda r, h: r.at[pl.ds(h * (C // 2), C // 2)],
            near2.at[c],
            far2.at[c],
            a,
            pos["ap"],
            pos["am"],
            red_ss,
            red_rs,
            12 * c + 6,
            step // 2,
        )
        second.describe()
        return first, second

    even_first, even_second = scatters(0)
    odd_first, odd_second = scatters(1)

    plan = {
        (0, 0): [(even.second_near, 0), (even.sibling, 0)],
        (0, 2): [(even.second_near, 1)],
        (0, 3): [(even.second_near, 2)],
        (1, 0): [(even.second_near, 3), (even.second_far, 0), (odd.first_near, 1), (even.sibling, 1)],
        (1, 1): [(odd.first_near, 2)],
        (1, 2): [(even.second_far, 1), (even.second_far, 2)],
        (1, 3): [(odd.second_near, 0)],
        (2, 0): [(odd.first_far,), (even.sibling, 2)],
        (2, 1): [(even.second_far, 3)],
        (2, 2): [(odd.second_near, 1)],
        (2, 3): [(odd.second_far, 0)],
        (3, 0): [(odd.second_near, 2), (even.sibling, 3)],
        (3, 2): [(odd.second_near, 3)],
        (3, 3): [(odd.second_far, 1)],
        (4, 0): [(even_first.start,), (odd.sibling, 0)],
        (4, 2): [(odd.second_far, 2)],
        (5, 0): [(odd.sibling, 1)],
        (5, 2): [(odd.second_far, 3)],
        (6, 0): [(odd.sibling, 2)],
        (6, 2): [(even_first.pass_on,)],
        (7, 0): [(odd.sibling, 3)],
    }

    def arrive(s, half):
        for (at, part), events in plan.items():
            if part == half:

                @pl.when(s == at)
                def _(events=events):
                    for event, *which in events:
                        event(*which)

    def expert_step(s, carry):
        c = s // 4
        off = ring_offset(s % 4)

        arrive(s, 0)
        g = (a0 + off) % 4

        def store_other(row, cols, total):
            tok[c, row, :, cols] = total.astype(BF16)

        experts(c, 1 - k, g, store_other, lambda: arrive(s, 1))
        hand_over(c, g, 1 - k).start()
        g = (b0 + off) % 4
        arrive(s, 2)

        def store_own(row, cols, total, g=g):
            sib[c, g, :, cols] = (total + sib[c, g, :, cols].astype(F32)).astype(BF16)

        def arrive_own(g=g):
            arrive(s, 3)
            hand_over(c, g, k).wait_recv()

        experts(c, k, g, store_own, arrive_own)
        return carry

    lax.fori_loop(0, 8, expert_step, 0)

    def last_rows(c, there):
        return sib.at[c, b0, pl.ds(pl.multiple_of(a0 * C + (there // 2) * R, R), R)]

    def last_copies(c, act):
        for there in range(c, nz, 2):

            @pl.when(z != there)
            def _(there=there):
                d = (there + nz - z) % nz
                act(z_copy(last_rows(c, there), zin2.at[d], there, last_ss, last_rs))

    odd_first.start()
    even_first.finish()
    even_second.start()
    odd_first.pass_on()
    even_second.pass_on()
    even_second.finish()
    last_copies(0, lambda copy: copy.start())
    odd_first.finish()
    odd_second.start()
    odd_second.pass_on()
    odd_second.finish()
    last_copies(1, lambda copy: copy.start())
    total = hid[...] + last_rows(z % 2, z)[...].astype(F32)
    for d in range(1, nz):
        z_copy(zin2.at[d], zin2.at[d], (z + d) % nz, last_ss, last_rs).wait_recv()
        total = total + zin2[d].astype(F32)
    out_ref[...] = total.astype(BF16)

    for scatter in (even_first, even_second, odd_first, odd_second):
        scatter.drain()
    for c in range(2):
        last_copies(c, lambda copy: copy.wait_send())
        for g in range(4):
            hand_over(c, g, 1 - k).wait_send()
    for there in order:

        @pl.when(z != there)
        def _(there=there):
            sum_copy(there).wait_send()

    for d in range(1, nz):
        z_copy(rows_at(z), rows_at(z), (z + d) % nz, row_ss, row_rs).wait_send()
    kv_gather.drain()
    even.drain()
    odd.drain()


def per_device(
    queries,
    key_rows,
    value_rows,
    residual,
    out_weight,
    norm_gain,
    gate_weight,
    up_weight,
    down_weight,
    routes,
    route_gates,
    block_picks,
):
    nz = lax.axis_size("exp")
    T, D = residual.shape
    R = T // nz
    C = T // 2
    F = gate_weight.shape[2]
    wide = -(-2 * F // 128) * 128
    cols = queries.shape[1]
    nh = cols // HD
    vmem = pl.BlockSpec(memory_space=pltpu.VMEM)
    anywhere = pl.BlockSpec(memory_space=pl.ANY)
    dma = pltpu.SemaphoreType.DMA
    return pl.pallas_call(
        functools.partial(kernel, nz),
        out_shape=jax.ShapeDtypeStruct((R, D), BF16),
        in_specs=[vmem] * 6 + [pl.BlockSpec(memory_space=pltpu.SMEM)] + [anywhere] * 5,
        out_specs=vmem,
        scratch_shapes=[
            pltpu.VMEM((8, 4, 2 * T + INFO, cols), BF16),
            pltpu.VMEM((2, 8, 4 * C, D), BF16),
            pltpu.VMEM((2, 4, 4 * C, D), BF16),
            pltpu.VMEM((2, 2, 4 * C, D), BF16),
            pltpu.VMEM((2, 2, 2 * C, D), BF16),
            pltpu.VMEM((2, 2, C, D), BF16),
            pltpu.VMEM((2, 2, C // 2, D), BF16),
            pltpu.VMEM((T, D), BF16),
            pltpu.VMEM((nz, R, D), BF16),
            pltpu.VMEM((nz, R, D), BF16),
            pltpu.VMEM((T, D), F32),
            pltpu.VMEM((R, D), F32),
            pltpu.VMEM((INFO, T), F32),
            pltpu.VMEM((R, D), BF16),
            pltpu.VMEM(out_weight.shape, BF16),
            pltpu.VMEM((2 * wide, D), BF16),
            pltpu.VMEM((wide, D), BF16),
            pltpu.VMEM((4 * C, wide), BF16),
            pltpu.VMEM((T, 128), F32),
            pltpu.VMEM((2, 8, 4 * C, 128), F32),
            pltpu.VMEM((nh, T, 128), F32),
            pltpu.VMEM((nh, T, 128), F32),
            pltpu.VMEM((nh, T, HD), F32),
            dma((8,)),
            dma((36,)),
            dma((36,)),
            dma((72,)),
            dma((72,)),
            dma((8,)),
            dma((8,)),
            dma((24,)),
            dma((24,)),
            dma((nz,)),
            dma((nz,)),
            dma((nz,)),
            dma((nz,)),
            dma((nz,)),
            dma((nz,)),
            pltpu.SemaphoreType.REGULAR((3,)),
        ],
        compiler_params=pltpu.CompilerParams(
            collective_id=0, has_side_effects=True, vmem_limit_bytes=60 * 1024 * 1024
        ),
        cost_estimate=pl.CostEstimate(flops=2 * 10**10, bytes_accessed=10**7, transcendentals=10**6),
    )(
        queries,
        key_rows,
        value_rows,
        routes.T,
        route_gates.T,
        norm_gain.reshape(1, D),
        block_picks.T,
        residual,
        out_weight,
        jnp.swapaxes(gate_weight, 1, 2),
        jnp.swapaxes(up_weight, 1, 2),
        down_weight,
    )


def solution(mesh):
    placed = (
        P("seq", "exp"),
        P("seq", "exp"),
        P("seq", "exp"),
        P("seq", None),
        P("exp", None),
        P(),
        P("seq", None, "exp"),
        P("seq", None, "exp"),
        P("seq", "exp", None),
        P("seq", None),
        P("seq", None),
        P(),
    )
    return jax.shard_map(
        per_device, mesh=mesh, in_specs=placed, out_specs=P(("seq", "exp"), None), check_vma=False
    )
```

```python
import functools

import jax
import jax.numpy as jnp
from jax import lax
from jax.experimental import pallas as pl
from jax.experimental.pallas import tpu as pltpu
from jax.sharding import PartitionSpec as P

HD = 128
TOPK = 6
BLK = 512
INFO = 32
MESH = pl.DeviceIdType.MESH
F32 = jnp.float32
BF16 = jnp.bfloat16


def ring_offset(step):
    return step // 2 + (step % 2) * (3 - 2 * (step // 2))


class Gather:
    def __init__(self, place, half, pos, send_sem, recv_sem, base=0, direct=False):
        self.place, self.half, self.pos = place, half, pos
        self.ss, self.rs, self.base, self.direct = send_sem, recv_sem, base, direct

    def send(self, ref, idx, dev):
        copy = pltpu.make_async_remote_copy(
            src_ref=ref,
            dst_ref=ref,
            send_sem=self.ss.at[self.base + idx],
            recv_sem=self.rs.at[self.base + idx],
            device_id={"seq": dev},
            device_id_type=MESH,
        )
        copy.start()

    def wait(self, ref, idx):
        pltpu.make_async_remote_copy(
            src_ref=ref,
            dst_ref=ref,
            send_sem=self.ss.at[self.base + idx],
            recv_sem=self.rs.at[self.base + idx],
            device_id={"seq": self.pos["sib"]},
            device_id_type=MESH,
        ).wait_recv()

    def wait_sent(self, ref, idx):
        pltpu.make_async_remote_copy(
            src_ref=ref,
            dst_ref=ref,
            send_sem=self.ss.at[self.base + idx],
            recv_sem=self.rs.at[self.base + idx],
            device_id={"seq": self.pos["sib"]},
            device_id_type=MESH,
        ).wait_send()

    def own_ready(self):
        p = self.pos
        block = self.place(p["k"], p["b"][0], p["a"][0])
        self.send(block, 0, p["ap"])
        self.send(block, 1, p["am"])
        if self.direct:
            self.send(block, 2, p["aa"])
        self.send(block, 4, p["bp"])
        self.send(block, 8, p["bm"])
        self.send(block, 20, p["sib"])

    def first_near(self, j):
        p = self.pos
        block = self.place(p["k"], p["b"][0], p["a"][j])
        self.wait(block, j - 1)
        if not self.direct:
            self.send(self.half(block, j - 1), 1 + j, p["ap"] if j == 1 else p["am"])
        self.send(block, 4 + j, p["bp"])
        self.send(block, 8 + j, p["bm"])
        self.send(block, 20 + j, p["sib"])

    def first_far(self):
        p = self.pos
        block = self.place(p["k"], p["b"][0], p["a"][3])
        if self.direct:
            self.wait(block, 2)
        else:
            self.wait(self.half(block, 0), 2)
            self.wait(self.half(block, 1), 3)
        self.send(block, 7, p["bp"])
        self.send(block, 11, p["bm"])
        self.send(block, 23, p["sib"])

    def second_near(self, j):
        p = self.pos
        block = self.place(p["k"], p["b"][1], p["a"][j])
        self.wait(block, 4 + j)
        self.send(self.half(block, 0), 12 + j, p["bp"])
        self.send(block, 24 + j, p["sib"])
        block = self.place(p["k"], p["b"][2], p["a"][j])
        self.wait(block, 8 + j)
        self.send(self.half(block, 1), 16 + j, p["bm"])
        self.send(block, 28 + j, p["sib"])

    def second_far(self, j):
        p = self.pos
        block = self.place(p["k"], p["b"][3], p["a"][j])
        self.wait(self.half(block, 0), 12 + j)
        self.wait(self.half(block, 1), 16 + j)
        self.send(block, 32 + j, p["sib"])

    def sibling(self, group):
        p = self.pos
        for j in range(4):
            block = self.place(1 - p["k"], p["a"][group], p["b"][j])
            self.wait(block, 20 + 4 * group + j)

    def drain(self):
        p = self.pos
        block = self.place(p["k"], p["b"][0], p["a"][0])
        for idx in range(36):
            if self.direct and idx == 3:
                continue
            halved = 12 <= idx < 20 or (idx in (2, 3) and not self.direct)
            part = self.half(block, 0) if halved else block
            self.wait_sent(part, idx)


def add_rows(dst, srcs, rows, step):
    def body(i, carry):
        at = pl.ds(pl.multiple_of(i * step, step), step)
        total = dst[at, :].astype(F32)
        for src in srcs:
            total = total + src[at, :].astype(F32)
        dst[at, :] = total.astype(dst.dtype)
        return carry

    lax.fori_loop(0, rows // step, body, 0)


class Scatter:
    def __init__(self, piece, half, near, far, ring, up, down, ss, rs, base, step):
        self.own, self.before, self.after, self.opposite = [piece(i) for i in ring]
        self.half, self.near, self.far = half, near, far
        self.up, self.down, self.step = up, down, step
        self.ss, self.rs, self.base = ss, rs, base
        self.copies = []

    def copy(self, src, dst, dev):
        at = self.base + len(self.copies)
        copy = pltpu.make_async_remote_copy(
            src_ref=src,
            dst_ref=dst,
            send_sem=self.ss.at[at],
            recv_sem=self.rs.at[at],
            device_id={"seq": dev},
            device_id_type=MESH,
        )
        self.copies.append(copy)

    def describe(self):
        half, near, far = self.half, self.near, self.far
        self.copy(half(self.opposite, 0), far.at[0], self.up)
        self.copy(half(self.opposite, 1), far.at[1], self.down)
        self.copy(half(self.after, 1), half(near.at[0], 1), self.up)
        self.copy(half(self.before, 0), half(near.at[1], 0), self.down)
        self.copy(half(self.after, 0), half(near.at[0], 0), self.up)
        self.copy(half(self.before, 1), half(near.at[1], 1), self.down)

    def start(self):
        for copy in self.copies[:4]:
            copy.start()

    def pass_on(self):
        rows = self.own.shape[0] // 2
        self.copies[0].wait_recv()
        add_rows(self.half(self.after, 0), [self.far.at[0]], rows, self.step)
        self.copies[4].start()
        self.copies[1].wait_recv()
        add_rows(self.half(self.before, 1), [self.far.at[1]], rows, self.step)
        self.copies[5].start()

    def finish(self):
        for copy in self.copies[2:]:
            copy.wait_recv()
        add_rows(self.own, [self.near.at[0], self.near.at[1]], self.own.shape[0], self.step)

    def drain(self):
        for copy in self.copies:
            copy.wait_send()


def kernel(
    nz,
    q_ref,
    k_ref,
    v_ref,
    routes_ref,
    gates_ref,
    gain_ref,
    picks_ref,
    res_hbm,
    wo_hbm,
    wg_hbm,
    wu_hbm,
    wd_hbm,
    out_ref,
    kv,
    tok,
    sib,
    near1,
    far1,
    near2,
    far2,
    zout,
    zin,
    zin2,
    cols_out,
    cols_in,
    cols_sum,
    cols_land,
    pf,
    hid,
    facts,
    res,
    wo,
    wgu,
    wd,
    inner,
    table,
    gates,
    mx,
    sm,
    acc,
    load_sem,
    kv_ss,
    kv_rs,
    tok_ss,
    tok_rs,
    sib_ss,
    sib_rs,
    red_ss,
    red_rs,
    sum_ss,
    sum_rs,
    row_ss,
    row_rs,
    last_ss,
    last_rs,
    col_ss,
    col_rs,
    plane_ss,
    plane_rs,
    told_sem,
):
    T, D = q_ref.shape[0], wo.shape[1]
    NH = q_ref.shape[1] // HD
    R = T // nz
    C = T // 2
    FF = wg_hbm.shape[1]
    WIDE = wd.shape[0]
    tile = D // 8
    DN = D - tile
    me = lax.axis_index("seq")
    z = lax.axis_index("exp")
    k = me % 2
    x = (me // 2) % 4
    y = me // 8
    a0 = x * (1 - k) + y * k
    b0 = y * (1 - k) + x * k
    offs = (0, 3, 1, 2)
    a = [(a0 + o) % 4 for o in offs]
    b = [(b0 + o) % 4 for o in offs]

    def seq_of(first, second):
        return first * (2 + 6 * k) + second * (8 - 6 * k) + k

    pos = dict(
        k=k,
        a=a,
        b=b,
        ap=seq_of(a[2], b0),
        am=seq_of(a[1], b0),
        aa=seq_of(a[3], b0),
        bp=seq_of(a0, b[2]),
        bm=seq_of(a0, b[1]),
        sib=me + 1 - 2 * k,
    )

    barrier = pltpu.get_barrier_semaphore()
    for name in ("ap", "am", "aa", "bp", "bm", "sib"):
        pl.semaphore_signal(barrier, inc=1, device_id={"seq": pos[name]}, device_id_type=MESH)
    around = ((z + 1) % nz, (z + nz - 1) % nz)
    for there in around:
        pl.semaphore_signal(barrier, inc=1, device_id={"exp": there}, device_id_type=MESH)

    own_kv = kv.at[k * 4 + b0, a0]
    own_kv[0:T, :] = k_ref[...]
    own_kv[T : 2 * T, :] = v_ref[...]
    gate = gates_ref[...]
    high = gate.astype(BF16).astype(F32)
    facts[...] = jnp.zeros(facts.shape, F32)
    facts[0:8, :] = jnp.full((8, T), -1.0, F32)
    facts[0:TOPK, :] = routes_ref[...].astype(F32)
    facts[8 : 8 + TOPK, :] = high
    facts[16 : 16 + TOPK, :] = gate - high
    own_kv[2 * T : 2 * T + INFO, 0:T] = facts[...].astype(BF16)
    own_kv[2 * T : 2 * T + INFO, T:] = jnp.zeros((INFO, own_kv.shape[1] - T), BF16)
    pl.semaphore_wait(barrier, 8)

    kv_half = kv.shape[2] // 2
    kv_gather = Gather(
        lambda kk, g, i: kv.at[kk * 4 + g, i],
        lambda block, h: block.at[pl.ds(h * kv_half, kv_half)],
        pos,
        kv_ss,
        kv_rs,
        direct=True,
    )
    kv_gather.own_ready()

    def tell(r):
        for there in around:
            pl.semaphore_signal(
                told_sem.at[r], inc=1, device_id={"exp": there}, device_id_type=MESH
            )

    def heard(r):
        pl.semaphore_wait(told_sem.at[r], 2)

    tell(0)
    loads = [
        pltpu.make_async_copy(src, dst, load_sem.at[i])
        for i, (src, dst) in enumerate(
            [
                (wo_hbm, wo),
                (res_hbm.at[pl.ds(pl.multiple_of(z * R, R), R)], res),
            ]
            + [(wg_hbm.at[e], wgu.at[e * FF : (e + 1) * FF]) for e in range(2)]
            + [(wu_hbm.at[e], wgu.at[WIDE + e * FF : WIDE + (e + 1) * FF]) for e in range(2)]
            + [(wd_hbm.at[e], wd.at[e * FF : (e + 1) * FF]) for e in range(2)]
        )
    ]
    for load in loads:
        load.start()
    spare = jnp.zeros((WIDE - 2 * FF, D), BF16)
    wgu[2 * FF : WIDE, :] = spare
    wgu[WIDE + 2 * FF : 2 * WIDE, :] = spare
    wd[2 * FF : WIDE, :] = spare
    mx[...] = jnp.full(mx.shape, -1e30, F32)
    sm[...] = jnp.zeros(sm.shape, F32)
    acc[...] = jnp.zeros(acc.shape, F32)

    kv_gather.first_near(1)
    kv_gather.first_near(2)
    heard(0)
    tell(1)
    kv_gather.first_far()
    heard(1)
    tell(2)

    per_block = BLK // 128
    mine = me // per_block
    picks = [picks_ref[i, mine] for i in range(picks_ref.shape[0])]
    scale = HD ** (-0.5)

    def attend(kk, g):
        row = kk * 4 + g
        col = lax.broadcasted_iota(jnp.int32, (1, 4 * T), 1)
        seq_key = (col // T) * (2 + 6 * kk) + (g * (8 - 6 * kk) + kk)
        key_block = seq_key // per_block
        named = key_block == picks[0]
        for pick in picks[1:]:
            named = named | (key_block == pick)
        key_pos = jnp.where(named, seq_key * T + col % T, jnp.int32(1 << 30))
        query_pos = me * T + lax.broadcasted_iota(jnp.int32, (T, 1), 0)
        allowed = key_pos <= query_pos
        for h in range(NH):
            cols = slice(h * HD, (h + 1) * HD)
            keys = kv[row, :, 0:T, cols].reshape(4 * T, HD)
            values = kv[row, :, T : 2 * T, cols].reshape(4 * T, HD)
            s = (
                lax.dot_general(
                    q_ref[:, cols], keys, (((1,), (1,)), ((), ())), preferred_element_type=F32
                )
                * scale
            )
            s = jnp.where(allowed, s, -1e30)
            old = mx[h]
            new = jnp.maximum(old, jnp.max(s, axis=1, keepdims=True))
            w = jnp.where(allowed, jnp.exp(s - new[:, 0:1]), 0.0)
            fade = jnp.exp(old - new)
            mx[h] = new
            sm[h] = sm[h] * fade + jnp.sum(w, axis=1, keepdims=True)
            acc[h] = acc[h] * fade + jnp.dot(w.astype(BF16), values, preferred_element_type=F32)

    def attend_step(i, carry):
        @pl.when(i == 0)
        def _():
            kv_gather.second_near(0)
            kv_gather.second_near(1)
            kv_gather.sibling(0)

        @pl.when(i == 1)
        def _():
            kv_gather.second_near(2)
            kv_gather.second_near(3)
            kv_gather.sibling(1)

        @pl.when(i == 2)
        def _():
            kv_gather.sibling(2)

        @pl.when(i == 3)
        def _():
            for j in range(4):
                kv_gather.second_far(j)
            kv_gather.sibling(3)

        off = ring_offset(i)
        attend(1 - k, (a0 + off) % 4)
        attend(k, (b0 + off) % 4)
        return carry

    lax.fori_loop(0, 4, attend_step, 0)

    loads[0].wait()
    for h in range(NH):
        head = (acc[h] / sm[h]).astype(BF16)
        term = jnp.dot(head, wo[h * HD : (h + 1) * HD, :], preferred_element_type=F32)
        pf[...] = term if h == 0 else pf[...] + term
    zout[...] = pf[...].astype(BF16)

    def z_copy(src, dst, there, ss, rs):
        d = (there + nz - z) % nz
        return pltpu.make_async_remote_copy(
            src_ref=src,
            dst_ref=dst,
            send_sem=ss.at[d],
            recv_sem=rs.at[d],
            device_id={"exp": there},
            device_id_type=MESH,
        )

    def rows_of(there):
        return pl.ds(pl.multiple_of(there * R, R), R)

    heard(2)

    def toward(parity, act):
        for m in (2, 1, 3, 0):
            if m < nz // 2:
                d = (parity + z) % 2 + 2 * m

                @pl.when(d > 0)
                def _(d=d):
                    act((z + d) % nz)

    def sum_copy(there):
        d = (there + nz - z) % nz
        return z_copy(zout.at[rows_of(there)], zin.at[d], there, sum_ss, sum_rs)

    for parity in range(2):
        toward(parity, lambda there: sum_copy(there).start())

    def gate_step(row, carry):
        for i in range(4):
            told = kv[row, i, 2 * T : 2 * T + INFO, 0:T].astype(F32)
            named, given = told[0:8], told[8:16] + told[16:24]
            lane = lax.broadcasted_iota(jnp.int32, (128, T), 0)
            grid = jnp.zeros((128, T), F32)
            for e in range(2):
                hit = named == (2 * me + e).astype(F32)
                worth = jnp.sum(jnp.where(hit, given, 0.0), axis=0, keepdims=True)
                grid = jnp.where(lane == e, worth, grid)
            table[...] = grid.T
            for there in range(nz):
                at = i * C + (there // 2) * R
                gates[there % 2, row, at : at + R, :] = table[there * R : (there + 1) * R, :]
        return carry

    lax.fori_loop(0, 8, gate_step, 0)
    loads[1].wait()
    hidden = res[...].astype(F32) + pf[rows_of(z), :]
    for d in range(1, nz):
        z_copy(zin.at[d], zin.at[d], (z + d) % nz, sum_ss, sum_rs).wait_recv()
        hidden = hidden + zin[d].astype(F32)
    mean_square = jnp.mean(hidden * hidden, axis=-1, keepdims=True)
    hid[...] = hidden
    normed = (hidden * lax.rsqrt(mean_square + 1e-06) * gain_ref[...]).astype(BF16)

    own_group = k * 4 + b0

    def rows_at(there):
        return tok.at[
            there % 2, own_group, pl.ds(pl.multiple_of(a0 * C + (there // 2) * R, R), R)
        ]

    rows_at(z)[...] = normed

    def spread():
        for d in (4, 3, 5, 2, 6, 1, 7):
            if d < nz:
                z_copy(rows_at(z), rows_at(z), (z + d) % nz, row_ss, row_rs).start()

    def spread_arrived(parity):
        for there in range(parity, nz, 2):

            @pl.when(z != there)
            def _(there=there):
                back = (z + nz - there) % nz
                z_copy(rows_at(there), rows_at(there), (z + back) % nz, row_ss, row_rs).wait_recv()

    @pl.when(z % 2 == 0)
    def _():
        spread()

    spread_arrived(0)

    @pl.when(z % 2 == 1)
    def _():
        spread()

    def gather_of(c):
        return Gather(
            lambda kk, g, i: tok.at[c, kk * 4 + g, pl.ds(pl.multiple_of(i * C, C), C)],
            lambda block, h: block.at[pl.ds(h * (C // 2), C // 2)],
            pos,
            tok_ss,
            tok_rs,
            36 * c,
            direct=c == 0,
        )

    even, odd = gather_of(0), gather_of(1)
    even.own_ready()
    for load in loads[2:]:
        load.wait()
    even.first_near(1)
    even.first_near(2)
    even.first_far()
    spread_arrived(1)
    odd.own_ready()

    def experts(c, kk, g, store, between):
        row = kk * 4 + g
        both = lax.dot_general(
            tok[c, row], wgu[...], (((1,), (1,)), ((), ())), preferred_element_type=F32
        )
        gate_part, up_part = both[:, 0:WIDE], both[:, WIDE : 2 * WIDE]
        lane = lax.broadcasted_iota(jnp.int32, (4 * C, WIDE), 1)
        worth = 0.5 * jnp.where(lane < FF, gates[c, row, :, 0:1], gates[c, row, :, 1:2])
        inner[...] = (gate_part * (1.0 + jnp.tanh(0.5 * gate_part)) * up_part * worth).astype(BF16)
        between()
        for t in range(D // tile):
            cols = slice(t * tile, (t + 1) * tile)
            store(row, cols, jnp.dot(inner[...], wd[:, cols], preferred_element_type=F32))

    def hand_over(c, g, kk):
        return pltpu.make_async_remote_copy(
            src_ref=tok.at[c, kk * 4 + g],
            dst_ref=sib.at[c, g],
            send_sem=sib_ss.at[c * 4 + g],
            recv_sem=sib_rs.at[c * 4 + g],
            device_id={"seq": pos["sib"]},
            device_id_type=MESH,
        )

    step = min(64, C // 2)

    def scatters(c):
        first = Scatter(
            lambda i: sib.at[c, i, :, 0:DN],
            lambda r, h: r.at[pl.ds(h * 2 * C, 2 * C)],
            near1.at[c],
            far1.at[c],
            b,
            pos["bp"],
            pos["bm"],
            red_ss,
            red_rs,
            12 * c,
            step,
        )
        first.describe()
        second = Scatter(
            lambda i: sib.at[c, b0, pl.ds(pl.multiple_of(i * C, C), C), 0:DN],
            lambda r, h: r.at[pl.ds(h * (C // 2), C // 2)],
            near2.at[c],
            far2.at[c],
            a,
            pos["ap"],
            pos["am"],
            red_ss,
            red_rs,
            12 * c + 6,
            step // 2,
        )
        second.describe()
        return first, second

    even_first, even_second = scatters(0)
    odd_first, odd_second = scatters(1)

    def column_copies(c, act):
        def one(there):
            d = (there + nz - z) % nz
            act(z_copy(cols_out.at[c, there // 2], cols_in.at[d], there, col_ss, col_rs))

        toward(c, one)

    def even_start():
        even_first.start()
        column_copies(0, lambda copy: copy.start())

    def plane_copies():
        return [
            pltpu.make_async_remote_copy(
                src_ref=cols_sum.at[b[j] * 4 + a[i]],
                dst_ref=cols_land.at[j * 4 + i],
                send_sem=plane_ss.at[j * 4 + i],
                recv_sem=plane_rs.at[j * 4 + i],
                device_id={"seq": seq_of(a[i], b[j])},
                device_id_type=MESH,
            )
            for j in range(4)
            for i in range(4)
            if i + j > 0
        ]

    def column_totals():
        for d in range(1, nz):
            z_copy(cols_in.at[d], cols_in.at[d], (z + d) % nz, col_ss, col_rs).wait_recv()

        def body(at, carry):
            total = cols_out[z % 2, z // 2, at].astype(F32)
            for d in range(1, nz):
                total = total + cols_in[d, at].astype(F32)
            cols_sum[at] = total.astype(BF16)
            return carry

        lax.fori_loop(0, 16, body, 0)
        for copy in plane_copies():
            copy.start()

    plan = {
        (0, 0): [(even.second_near, 0), (even.sibling, 0)],
        (0, 2): [(even.second_near, 1)],
        (0, 3): [(even.second_near, 2)],
        (1, 0): [(even.second_near, 3), (even.second_far, 0), (odd.first_near, 1), (even.sibling, 1)],
        (1, 1): [(odd.first_near, 2)],
        (1, 2): [(even.second_far, 1), (even.second_far, 2)],
        (1, 3): [(odd.second_near, 0)],
        (2, 0): [(odd.first_far,), (even.sibling, 2)],
        (2, 1): [(even.second_far, 3)],
        (2, 2): [(odd.second_near, 1)],
        (2, 3): [(odd.second_far, 0)],
        (3, 0): [(odd.second_near, 2), (even.sibling, 3)],
        (3, 2): [(odd.second_near, 3)],
        (3, 3): [(odd.second_far, 1)],
        (4, 0): [(even_start,), (odd.sibling, 0)],
        (4, 2): [(odd.second_far, 2)],
        (5, 0): [(odd.sibling, 1)],
        (5, 2): [(odd.second_far, 3)],
        (6, 0): [(odd.sibling, 2)],
        (6, 2): [(even_first.pass_on,)],
        (7, 0): [(odd.sibling, 3)],
    }

    def arrive(s, half):
        for (at, part), events in plan.items():
            if part == half:

                @pl.when(s == at)
                def _(events=events):
                    for event, *which in events:
                        event(*which)

    def expert_step(s, carry):
        c = s // 4
        off = ring_offset(s % 4)

        arrive(s, 0)
        g = (a0 + off) % 4

        def store_other(row, cols, total):
            tok[c, row, :, cols] = total.astype(BF16)

        experts(c, 1 - k, g, store_other, lambda: arrive(s, 1))
        hand_over(c, g, 1 - k).start()
        g = (b0 + off) % 4
        arrive(s, 2)

        def store_own(row, cols, total, g=g):
            value = (total + sib[c, g, :, cols].astype(F32)).astype(BF16)
            if cols.start < DN:
                sib[c, g, :, cols] = value
                return
            for i in range(4):
                for m in range(nz // 2):
                    at = i * C + m * R
                    cols_out[c, m, g * 4 + i] = value[at : at + R, :]

        def arrive_own(g=g):
            arrive(s, 3)
            hand_over(c, g, k).wait_recv()

        experts(c, k, g, store_own, arrive_own)
        return carry

    lax.fori_loop(0, 8, expert_step, 0)

    def last_rows(c, there):
        return sib.at[c, b0, pl.ds(pl.multiple_of(a0 * C + (there // 2) * R, R), R), 0:DN]

    def last_copies(c, act):
        def one(there):
            d = (there + nz - z) % nz
            act(z_copy(last_rows(c, there), zin2.at[d], there, last_ss, last_rs))

        toward(c, one)

    odd_first.start()
    column_copies(1, lambda copy: copy.start())
    even_first.finish()
    even_second.start()
    odd_first.pass_on()
    even_second.pass_on()
    even_second.finish()
    last_copies(0, lambda copy: copy.start())
    odd_first.finish()
    odd_second.start()
    odd_second.pass_on()
    odd_second.finish()
    last_copies(1, lambda copy: copy.start())
    column_totals()
    across = plane_copies()
    total = hid[:, DN:] + cols_sum[b0 * 4 + a0].astype(F32)
    for at, copy in enumerate(across):
        copy.wait_recv()
        total = total + cols_land[at + 1].astype(F32)
    out_ref[:, DN:] = total.astype(BF16)
    total = hid[:, 0:DN] + last_rows(z % 2, z)[...].astype(F32)
    for d in range(1, nz):
        z_copy(zin2.at[d], zin2.at[d], (z + d) % nz, last_ss, last_rs).wait_recv()
        total = total + zin2[d].astype(F32)
    out_ref[:, 0:DN] = total.astype(BF16)

    for scatter in (even_first, even_second, odd_first, odd_second):
        scatter.drain()
    for c in range(2):
        last_copies(c, lambda copy: copy.wait_send())
        column_copies(c, lambda copy: copy.wait_send())
        for g in range(4):
            hand_over(c, g, 1 - k).wait_send()
    for parity in range(2):
        toward(parity, lambda there: sum_copy(there).wait_send())

    for d in range(1, nz):
        z_copy(rows_at(z), rows_at(z), (z + d) % nz, row_ss, row_rs).wait_send()
    for copy in across:
        copy.wait_send()
    kv_gather.drain()
    even.drain()
    odd.drain()


def per_device(
    queries,
    key_rows,
    value_rows,
    residual,
    out_weight,
    norm_gain,
    gate_weight,
    up_weight,
    down_weight,
    routes,
    route_gates,
    block_picks,
):
    nz = lax.axis_size("exp")
    T, D = residual.shape
    R = T // nz
    C = T // 2
    tile = D // 8
    F = gate_weight.shape[2]
    wide = -(-2 * F // 128) * 128
    cols = queries.shape[1]
    nh = cols // HD
    vmem = pl.BlockSpec(memory_space=pltpu.VMEM)
    anywhere = pl.BlockSpec(memory_space=pl.ANY)
    dma = pltpu.SemaphoreType.DMA
    return pl.pallas_call(
        functools.partial(kernel, nz),
        out_shape=jax.ShapeDtypeStruct((R, D), BF16),
        in_specs=[vmem] * 6 + [pl.BlockSpec(memory_space=pltpu.SMEM)] + [anywhere] * 5,
        out_specs=vmem,
        scratch_shapes=[
            pltpu.VMEM((8, 4, 2 * T + INFO, cols), BF16),
            pltpu.VMEM((2, 8, 4 * C, D), BF16),
            pltpu.VMEM((2, 4, 4 * C, D), BF16),
            pltpu.VMEM((2, 2, 4 * C, D - tile), BF16),
            pltpu.VMEM((2, 2, 2 * C, D - tile), BF16),
            pltpu.VMEM((2, 2, C, D - tile), BF16),
            pltpu.VMEM((2, 2, C // 2, D - tile), BF16),
            pltpu.VMEM((T, D), BF16),
            pltpu.VMEM((nz, R, D), BF16),
            pltpu.VMEM((nz, R, D - tile), BF16),
            pltpu.VMEM((2, nz // 2, 16, R, tile), BF16),
            pltpu.VMEM((nz, 16, R, tile), BF16),
            pltpu.VMEM((16, R, tile), BF16),
            pltpu.VMEM((16, R, tile), BF16),
            pltpu.VMEM((T, D), F32),
            pltpu.VMEM((R, D), F32),
            pltpu.VMEM((INFO, T), F32),
            pltpu.VMEM((R, D), BF16),
            pltpu.VMEM(out_weight.shape, BF16),
            pltpu.VMEM((2 * wide, D), BF16),
            pltpu.VMEM((wide, D), BF16),
            pltpu.VMEM((4 * C, wide), BF16),
            pltpu.VMEM((T, 128), F32),
            pltpu.VMEM((2, 8, 4 * C, 128), F32),
            pltpu.VMEM((nh, T, 128), F32),
            pltpu.VMEM((nh, T, 128), F32),
            pltpu.VMEM((nh, T, HD), F32),
            dma((8,)),
            dma((36,)),
            dma((36,)),
            dma((72,)),
            dma((72,)),
            dma((8,)),
            dma((8,)),
            dma((24,)),
            dma((24,)),
            dma((nz,)),
            dma((nz,)),
            dma((nz,)),
            dma((nz,)),
            dma((nz,)),
            dma((nz,)),
            dma((nz,)),
            dma((nz,)),
            dma((16,)),
            dma((16,)),
            pltpu.SemaphoreType.REGULAR((3,)),
        ],
        compiler_params=pltpu.CompilerParams(
            collective_id=0, has_side_effects=True, vmem_limit_bytes=60 * 1024 * 1024
        ),
        cost_estimate=pl.CostEstimate(flops=2 * 10**10, bytes_accessed=10**7, transcendentals=10**6),
    )(
        queries,
        key_rows,
        value_rows,
        routes.T,
        route_gates.T,
        norm_gain.reshape(1, D),
        block_picks.T,
        residual,
        out_weight,
        jnp.swapaxes(gate_weight, 1, 2),
        jnp.swapaxes(up_weight, 1, 2),
        down_weight,
    )


def solution(mesh):
    placed = (
        P("seq", "exp"),
        P("seq", "exp"),
        P("seq", "exp"),
        P("seq", None),
        P("exp", None),
        P(),
        P("seq", None, "exp"),
        P("seq", None, "exp"),
        P("seq", "exp", None),
        P("seq", None),
        P("seq", None),
        P(),
    )
    return jax.shard_map(
        per_device, mesh=mesh, in_specs=placed, out_specs=P(("seq", "exp"), None), check_vma=False
    )
```

```python
import functools

import jax
import jax.numpy as jnp
from jax import lax
from jax.experimental import pallas as pl
from jax.experimental.pallas import tpu as pltpu
from jax.sharding import PartitionSpec as P

HD = 128
TOPK = 6
BLK = 512
INFO = 32
MESH = pl.DeviceIdType.MESH
F32 = jnp.float32
BF16 = jnp.bfloat16


def ring_offset(step):
    return step // 2 + (step % 2) * (3 - 2 * (step // 2))


class Gather:
    def __init__(self, place, half, pos, send_sem, recv_sem, base=0, direct=False):
        self.place, self.half, self.pos = place, half, pos
        self.ss, self.rs, self.base, self.direct = send_sem, recv_sem, base, direct

    def send(self, ref, idx, dev):
        copy = pltpu.make_async_remote_copy(
            src_ref=ref,
            dst_ref=ref,
            send_sem=self.ss.at[self.base + idx],
            recv_sem=self.rs.at[self.base + idx],
            device_id={"seq": dev},
            device_id_type=MESH,
        )
        copy.start()

    def wait(self, ref, idx):
        pltpu.make_async_remote_copy(
            src_ref=ref,
            dst_ref=ref,
            send_sem=self.ss.at[self.base + idx],
            recv_sem=self.rs.at[self.base + idx],
            device_id={"seq": self.pos["sib"]},
            device_id_type=MESH,
        ).wait_recv()

    def wait_sent(self, ref, idx):
        pltpu.make_async_remote_copy(
            src_ref=ref,
            dst_ref=ref,
            send_sem=self.ss.at[self.base + idx],
            recv_sem=self.rs.at[self.base + idx],
            device_id={"seq": self.pos["sib"]},
            device_id_type=MESH,
        ).wait_send()

    def own_ready(self):
        p = self.pos
        block = self.place(p["k"], p["b"][0], p["a"][0])
        self.send(block, 0, p["ap"])
        self.send(block, 1, p["am"])
        if self.direct:
            self.send(block, 2, p["aa"])
        self.send(block, 4, p["bp"])
        self.send(block, 8, p["bm"])
        self.send(block, 20, p["sib"])

    def first_near(self, j):
        p = self.pos
        block = self.place(p["k"], p["b"][0], p["a"][j])
        self.wait(block, j - 1)
        if not self.direct:
            self.send(self.half(block, j - 1), 1 + j, p["ap"] if j == 1 else p["am"])
        self.send(block, 4 + j, p["bp"])
        self.send(block, 8 + j, p["bm"])
        self.send(block, 20 + j, p["sib"])

    def first_far(self):
        p = self.pos
        block = self.place(p["k"], p["b"][0], p["a"][3])
        if self.direct:
            self.wait(block, 2)
        else:
            self.wait(self.half(block, 0), 2)
            self.wait(self.half(block, 1), 3)
        self.send(block, 7, p["bp"])
        self.send(block, 11, p["bm"])
        self.send(block, 23, p["sib"])

    def second_near(self, j):
        p = self.pos
        block = self.place(p["k"], p["b"][1], p["a"][j])
        self.wait(block, 4 + j)
        self.send(self.half(block, 0), 12 + j, p["bp"])
        self.send(block, 24 + j, p["sib"])
        block = self.place(p["k"], p["b"][2], p["a"][j])
        self.wait(block, 8 + j)
        self.send(self.half(block, 1), 16 + j, p["bm"])
        self.send(block, 28 + j, p["sib"])

    def second_far(self, j):
        p = self.pos
        block = self.place(p["k"], p["b"][3], p["a"][j])
        self.wait(self.half(block, 0), 12 + j)
        self.wait(self.half(block, 1), 16 + j)
        self.send(block, 32 + j, p["sib"])

    def sibling(self, group):
        p = self.pos
        for j in range(4):
            block = self.place(1 - p["k"], p["a"][group], p["b"][j])
            self.wait(block, 20 + 4 * group + j)

    def drain(self):
        p = self.pos
        block = self.place(p["k"], p["b"][0], p["a"][0])
        for idx in range(36):
            if self.direct and idx == 3:
                continue
            halved = 12 <= idx < 20 or (idx in (2, 3) and not self.direct)
            part = self.half(block, 0) if halved else block
            self.wait_sent(part, idx)


def add_rows(dst, srcs, rows, step):
    def body(i, carry):
        at = pl.ds(pl.multiple_of(i * step, step), step)
        total = dst[at, :].astype(F32)
        for src in srcs:
            total = total + src[at, :].astype(F32)
        dst[at, :] = total.astype(dst.dtype)
        return carry

    lax.fori_loop(0, rows // step, body, 0)


class Scatter:
    def __init__(self, piece, half, near, far, ring, up, down, ss, rs, base, step):
        self.own, self.before, self.after, self.opposite = [piece(i) for i in ring]
        self.half, self.near, self.far = half, near, far
        self.up, self.down, self.step = up, down, step
        self.ss, self.rs, self.base = ss, rs, base
        self.copies = []

    def copy(self, src, dst, dev):
        at = self.base + len(self.copies)
        copy = pltpu.make_async_remote_copy(
            src_ref=src,
            dst_ref=dst,
            send_sem=self.ss.at[at],
            recv_sem=self.rs.at[at],
            device_id={"seq": dev},
            device_id_type=MESH,
        )
        self.copies.append(copy)

    def describe(self):
        half, near, far = self.half, self.near, self.far
        self.copy(half(self.opposite, 0), far.at[0], self.up)
        self.copy(half(self.opposite, 1), far.at[1], self.down)
        self.copy(half(self.after, 1), half(near.at[0], 1), self.up)
        self.copy(half(self.before, 0), half(near.at[1], 0), self.down)
        self.copy(half(self.after, 0), half(near.at[0], 0), self.up)
        self.copy(half(self.before, 1), half(near.at[1], 1), self.down)

    def start_far(self):
        for copy in self.copies[:2]:
            copy.start()

    def start_near(self):
        for copy in self.copies[2:4]:
            copy.start()

    def start(self):
        self.start_far()
        self.start_near()

    def pass_on(self):
        rows = self.own.shape[0] // 2
        self.copies[0].wait_recv()
        add_rows(self.half(self.after, 0), [self.far.at[0]], rows, self.step)
        self.copies[4].start()
        self.copies[1].wait_recv()
        add_rows(self.half(self.before, 1), [self.far.at[1]], rows, self.step)
        self.copies[5].start()

    def finish(self):
        for copy in self.copies[2:]:
            copy.wait_recv()
        add_rows(self.own, [self.near.at[0], self.near.at[1]], self.own.shape[0], self.step)

    def drain(self):
        for copy in self.copies:
            copy.wait_send()


def kernel(
    nz,
    q_ref,
    k_ref,
    v_ref,
    routes_ref,
    gates_ref,
    gain_ref,
    picks_ref,
    res_hbm,
    wo_hbm,
    wg_hbm,
    wu_hbm,
    wd_hbm,
    out_ref,
    kv,
    tok,
    sib,
    near1,
    far1,
    near2,
    far2,
    zout,
    zin,
    zin2,
    cols_out,
    cols_in,
    cols_sum,
    cols_land,
    pf,
    hid,
    facts,
    res,
    wo,
    wgu,
    wd,
    inner,
    table,
    gates,
    mx,
    sm,
    acc,
    load_sem,
    kv_ss,
    kv_rs,
    tok_ss,
    tok_rs,
    sib_ss,
    sib_rs,
    red_ss,
    red_rs,
    sum_ss,
    sum_rs,
    row_ss,
    row_rs,
    last_ss,
    last_rs,
    col_ss,
    col_rs,
    plane_ss,
    plane_rs,
    told_sem,
):
    T, D = q_ref.shape[0], wo.shape[1]
    NH = q_ref.shape[1] // HD
    R = T // nz
    C = T // 2
    FF = wg_hbm.shape[1]
    WIDE = wd.shape[0]
    tile = D // 8
    DN = D - tile
    me = lax.axis_index("seq")
    z = lax.axis_index("exp")
    k = me % 2
    x = (me // 2) % 4
    y = me // 8
    a0 = x * (1 - k) + y * k
    b0 = y * (1 - k) + x * k
    offs = (0, 3, 1, 2)
    a = [(a0 + o) % 4 for o in offs]
    b = [(b0 + o) % 4 for o in offs]

    def seq_of(first, second):
        return first * (2 + 6 * k) + second * (8 - 6 * k) + k

    pos = dict(
        k=k,
        a=a,
        b=b,
        ap=seq_of(a[2], b0),
        am=seq_of(a[1], b0),
        aa=seq_of(a[3], b0),
        bp=seq_of(a0, b[2]),
        bm=seq_of(a0, b[1]),
        sib=me + 1 - 2 * k,
    )

    barrier = pltpu.get_barrier_semaphore()
    for name in ("ap", "am", "aa", "bp", "bm", "sib"):
        pl.semaphore_signal(barrier, inc=1, device_id={"seq": pos[name]}, device_id_type=MESH)
    around = ((z + 1) % nz, (z + nz - 1) % nz)
    for there in around:
        pl.semaphore_signal(barrier, inc=1, device_id={"exp": there}, device_id_type=MESH)

    own_kv = kv.at[k * 4 + b0, a0]
    own_kv[0:T, :] = k_ref[...]
    own_kv[T : 2 * T, :] = v_ref[...]
    gate = gates_ref[...]
    high = gate.astype(BF16).astype(F32)
    facts[...] = jnp.zeros(facts.shape, F32)
    facts[0:8, :] = jnp.full((8, T), -1.0, F32)
    facts[0:TOPK, :] = routes_ref[...].astype(F32)
    facts[8 : 8 + TOPK, :] = high
    facts[16 : 16 + TOPK, :] = gate - high
    own_kv[2 * T : 2 * T + INFO, 0:T] = facts[...].astype(BF16)
    own_kv[2 * T : 2 * T + INFO, T:] = jnp.zeros((INFO, own_kv.shape[1] - T), BF16)
    pl.semaphore_wait(barrier, 8)

    kv_half = kv.shape[2] // 2
    kv_gather = Gather(
        lambda kk, g, i: kv.at[kk * 4 + g, i],
        lambda block, h: block.at[pl.ds(h * kv_half, kv_half)],
        pos,
        kv_ss,
        kv_rs,
        direct=True,
    )
    kv_gather.own_ready()

    def tell(r):
        for there in around:
            pl.semaphore_signal(
                told_sem.at[r], inc=1, device_id={"exp": there}, device_id_type=MESH
            )

    def heard(r):
        pl.semaphore_wait(told_sem.at[r], 2)

    tell(0)
    loads = [
        pltpu.make_async_copy(src, dst, load_sem.at[i])
        for i, (src, dst) in enumerate(
            [
                (wo_hbm, wo),
                (res_hbm.at[pl.ds(pl.multiple_of(z * R, R), R)], res),
            ]
            + [(wg_hbm.at[e], wgu.at[e * FF : (e + 1) * FF]) for e in range(2)]
            + [(wu_hbm.at[e], wgu.at[WIDE + e * FF : WIDE + (e + 1) * FF]) for e in range(2)]
            + [(wd_hbm.at[e], wd.at[e * FF : (e + 1) * FF]) for e in range(2)]
        )
    ]
    for load in loads:
        load.start()
    spare = jnp.zeros((WIDE - 2 * FF, D), BF16)
    wgu[2 * FF : WIDE, :] = spare
    wgu[WIDE + 2 * FF : 2 * WIDE, :] = spare
    wd[2 * FF : WIDE, :] = spare
    mx[...] = jnp.full(mx.shape, -1e30, F32)
    sm[...] = jnp.zeros(sm.shape, F32)
    acc[...] = jnp.zeros(acc.shape, F32)

    kv_gather.first_near(1)
    kv_gather.first_near(2)
    heard(0)
    tell(1)
    kv_gather.first_far()
    heard(1)
    tell(2)

    per_block = BLK // 128
    mine = me // per_block
    picks = [picks_ref[i, mine] for i in range(picks_ref.shape[0])]
    scale = HD ** (-0.5)

    def attend(kk, g):
        row = kk * 4 + g
        col = lax.broadcasted_iota(jnp.int32, (1, 4 * T), 1)
        seq_key = (col // T) * (2 + 6 * kk) + (g * (8 - 6 * kk) + kk)
        key_block = seq_key // per_block
        named = key_block == picks[0]
        for pick in picks[1:]:
            named = named | (key_block == pick)
        key_pos = jnp.where(named, seq_key * T + col % T, jnp.int32(1 << 30))
        query_pos = me * T + lax.broadcasted_iota(jnp.int32, (T, 1), 0)
        allowed = key_pos <= query_pos
        for h in range(NH):
            cols = slice(h * HD, (h + 1) * HD)
            keys = kv[row, :, 0:T, cols].reshape(4 * T, HD)
            values = kv[row, :, T : 2 * T, cols].reshape(4 * T, HD)
            s = (
                lax.dot_general(
                    q_ref[:, cols], keys, (((1,), (1,)), ((), ())), preferred_element_type=F32
                )
                * scale
            )
            s = jnp.where(allowed, s, -1e30)
            old = mx[h]
            new = jnp.maximum(old, jnp.max(s, axis=1, keepdims=True))
            w = jnp.where(allowed, jnp.exp(s - new[:, 0:1]), 0.0)
            fade = jnp.exp(old - new)
            mx[h] = new
            sm[h] = sm[h] * fade + jnp.sum(w, axis=1, keepdims=True)
            acc[h] = acc[h] * fade + jnp.dot(w.astype(BF16), values, preferred_element_type=F32)

    def attend_step(i, carry):
        @pl.when(i == 0)
        def _():
            kv_gather.second_near(0)
            kv_gather.second_near(1)
            kv_gather.sibling(0)

        @pl.when(i == 1)
        def _():
            kv_gather.second_near(2)
            kv_gather.second_near(3)
            kv_gather.sibling(1)

        @pl.when(i == 2)
        def _():
            kv_gather.sibling(2)

        @pl.when(i == 3)
        def _():
            for j in range(4):
                kv_gather.second_far(j)
            kv_gather.sibling(3)

        off = ring_offset(i)
        attend(1 - k, (a0 + off) % 4)
        attend(k, (b0 + off) % 4)
        return carry

    lax.fori_loop(0, 4, attend_step, 0)

    loads[0].wait()
    for h in range(NH):
        head = (acc[h] / sm[h]).astype(BF16)
        term = jnp.dot(head, wo[h * HD : (h + 1) * HD, :], preferred_element_type=F32)
        pf[...] = term if h == 0 else pf[...] + term
    zout[...] = pf[...].astype(BF16)

    def z_copy(src, dst, there, ss, rs):
        d = (there + nz - z) % nz
        return pltpu.make_async_remote_copy(
            src_ref=src,
            dst_ref=dst,
            send_sem=ss.at[d],
            recv_sem=rs.at[d],
            device_id={"exp": there},
            device_id_type=MESH,
        )

    def rows_of(there):
        return pl.ds(pl.multiple_of(there * R, R), R)

    heard(2)

    def toward(parity, act):
        for m in (2, 1, 3, 0):
            if m < nz // 2:
                d = (parity + z) % 2 + 2 * m

                @pl.when(d > 0)
                def _(d=d):
                    act((z + d) % nz)

    def sum_copy(there):
        d = (there + nz - z) % nz
        return z_copy(zout.at[rows_of(there)], zin.at[d], there, sum_ss, sum_rs)

    for parity in range(2):
        toward(parity, lambda there: sum_copy(there).start())

    def gate_step(row, carry):
        for i in range(4):
            told = kv[row, i, 2 * T : 2 * T + INFO, 0:T].astype(F32)
            named, given = told[0:8], told[8:16] + told[16:24]
            lane = lax.broadcasted_iota(jnp.int32, (128, T), 0)
            grid = jnp.zeros((128, T), F32)
            for e in range(2):
                hit = named == (2 * me + e).astype(F32)
                worth = jnp.sum(jnp.where(hit, given, 0.0), axis=0, keepdims=True)
                grid = jnp.where(lane == e, worth, grid)
            table[...] = grid.T
            for there in range(nz):
                at = i * C + (there // 2) * R
                gates[there % 2, row, at : at + R, :] = table[there * R : (there + 1) * R, :]
        return carry

    lax.fori_loop(0, 8, gate_step, 0)
    loads[1].wait()
    hidden = res[...].astype(F32) + pf[rows_of(z), :]
    for d in range(1, nz):
        z_copy(zin.at[d], zin.at[d], (z + d) % nz, sum_ss, sum_rs).wait_recv()
        hidden = hidden + zin[d].astype(F32)
    mean_square = jnp.mean(hidden * hidden, axis=-1, keepdims=True)
    hid[...] = hidden
    normed = (hidden * lax.rsqrt(mean_square + 1e-06) * gain_ref[...]).astype(BF16)

    own_group = k * 4 + b0

    def rows_at(there):
        return tok.at[
            there % 2, own_group, pl.ds(pl.multiple_of(a0 * C + (there // 2) * R, R), R)
        ]

    rows_at(z)[...] = normed

    def spread():
        for d in (4, 3, 5, 2, 6, 1, 7):
            if d < nz:
                z_copy(rows_at(z), rows_at(z), (z + d) % nz, row_ss, row_rs).start()

    def spread_arrived(parity):
        for there in range(parity, nz, 2):

            @pl.when(z != there)
            def _(there=there):
                back = (z + nz - there) % nz
                z_copy(rows_at(there), rows_at(there), (z + back) % nz, row_ss, row_rs).wait_recv()

    @pl.when(z % 2 == 0)
    def _():
        spread()

    spread_arrived(0)

    @pl.when(z % 2 == 1)
    def _():
        spread()

    def gather_of(c):
        return Gather(
            lambda kk, g, i: tok.at[c, kk * 4 + g, pl.ds(pl.multiple_of(i * C, C), C)],
            lambda block, h: block.at[pl.ds(h * (C // 2), C // 2)],
            pos,
            tok_ss,
            tok_rs,
            36 * c,
            direct=c == 0,
        )

    even, odd = gather_of(0), gather_of(1)
    even.own_ready()
    for load in loads[2:]:
        load.wait()
    even.first_near(1)
    even.first_near(2)
    even.first_far()
    spread_arrived(1)
    odd.own_ready()

    def experts(c, kk, g, store, between):
        row = kk * 4 + g
        both = lax.dot_general(
            tok[c, row], wgu[...], (((1,), (1,)), ((), ())), preferred_element_type=F32
        )
        gate_part, up_part = both[:, 0:WIDE], both[:, WIDE : 2 * WIDE]
        lane = lax.broadcasted_iota(jnp.int32, (4 * C, WIDE), 1)
        worth = 0.5 * jnp.where(lane < FF, gates[c, row, :, 0:1], gates[c, row, :, 1:2])
        inner[...] = (gate_part * (1.0 + jnp.tanh(0.5 * gate_part)) * up_part * worth).astype(BF16)
        between()
        for t in range(D // tile):
            cols = slice(t * tile, (t + 1) * tile)
            store(row, cols, jnp.dot(inner[...], wd[:, cols], preferred_element_type=F32))

    def hand_over(c, g, kk):
        return pltpu.make_async_remote_copy(
            src_ref=tok.at[c, kk * 4 + g],
            dst_ref=sib.at[c, g],
            send_sem=sib_ss.at[c * 4 + g],
            recv_sem=sib_rs.at[c * 4 + g],
            device_id={"seq": pos["sib"]},
            device_id_type=MESH,
        )

    step = min(64, C // 2)

    def scatters(c):
        first = Scatter(
            lambda i: sib.at[c, i, :, 0:DN],
            lambda r, h: r.at[pl.ds(h * 2 * C, 2 * C)],
            near1.at[c],
            far1.at[c],
            b,
            pos["bp"],
            pos["bm"],
            red_ss,
            red_rs,
            12 * c,
            step,
        )
        first.describe()
        second = Scatter(
            lambda i: sib.at[c, b0, pl.ds(pl.multiple_of(i * C, C), C), 0:DN],
            lambda r, h: r.at[pl.ds(h * (C // 2), C // 2)],
            near2.at[c],
            far2.at[c],
            a,
            pos["ap"],
            pos["am"],
            red_ss,
            red_rs,
            12 * c + 6,
            step // 2,
        )
        second.describe()
        return first, second

    even_first, even_second = scatters(0)
    odd_first, odd_second = scatters(1)

    def column_copies(c, act):
        def one(there):
            d = (there + nz - z) % nz
            act(z_copy(cols_out.at[c, there // 2], cols_in.at[d], there, col_ss, col_rs))

        toward(c, one)

    def even_start():
        even_first.start_far()
        column_copies(0, lambda copy: copy.start())

    def plane_copies():
        return [
            pltpu.make_async_remote_copy(
                src_ref=cols_sum.at[b[j] * 4 + a[i]],
                dst_ref=cols_land.at[j * 4 + i],
                send_sem=plane_ss.at[j * 4 + i],
                recv_sem=plane_rs.at[j * 4 + i],
                device_id={"seq": seq_of(a[i], b[j])},
                device_id_type=MESH,
            )
            for j in range(4)
            for i in range(4)
            if i + j > 0
        ]

    def column_totals():
        for d in range(1, nz):
            z_copy(cols_in.at[d], cols_in.at[d], (z + d) % nz, col_ss, col_rs).wait_recv()

        def body(at, carry):
            total = cols_out[z % 2, z // 2, at].astype(F32)
            for d in range(1, nz):
                total = total + cols_in[d, at].astype(F32)
            cols_sum[at] = total.astype(BF16)
            return carry

        lax.fori_loop(0, 16, body, 0)
        for copy in plane_copies():
            copy.start()

    plan = {
        (0, 0): [(even.second_near, 0), (even.sibling, 0)],
        (0, 2): [(even.second_near, 1)],
        (0, 3): [(even.second_near, 2)],
        (1, 0): [(even.second_near, 3), (even.second_far, 0), (odd.first_near, 1), (even.sibling, 1)],
        (1, 1): [(odd.first_near, 2)],
        (1, 2): [(even.second_far, 1), (even.second_far, 2)],
        (1, 3): [(odd.second_near, 0)],
        (2, 0): [(odd.first_far,), (even.sibling, 2)],
        (2, 1): [(even.second_far, 3)],
        (2, 2): [(odd.second_near, 1)],
        (2, 3): [(odd.second_far, 0)],
        (3, 0): [(odd.second_near, 2), (even.sibling, 3), (even_first.start_near,)],
        (3, 2): [(odd.second_near, 3)],
        (3, 3): [(odd.second_far, 1)],
        (4, 0): [(even_start,), (odd.sibling, 0)],
        (4, 2): [(odd.second_far, 2)],
        (5, 0): [(odd.sibling, 1)],
        (5, 2): [(odd.second_far, 3)],
        (6, 0): [(odd.sibling, 2)],
        (6, 2): [(even_first.pass_on,)],
        (7, 0): [(odd_first.start_near,), (odd.sibling, 3)],
    }

    def arrive(s, half):
        for (at, part), events in plan.items():
            if part == half:

                @pl.when(s == at)
                def _(events=events):
                    for event, *which in events:
                        event(*which)

    def expert_step(s, carry):
        c = s // 4
        off = ring_offset(s % 4)

        arrive(s, 0)
        g = (a0 + off) % 4

        def store_other(row, cols, total):
            tok[c, row, :, cols] = total.astype(BF16)

        experts(c, 1 - k, g, store_other, lambda: arrive(s, 1))
        hand_over(c, g, 1 - k).start()
        g = (b0 + off) % 4
        arrive(s, 2)

        def store_own(row, cols, total, g=g):
            value = (total + sib[c, g, :, cols].astype(F32)).astype(BF16)
            if cols.start < DN:
                sib[c, g, :, cols] = value
                return
            for i in range(4):
                for m in range(nz // 2):
                    at = i * C + m * R
                    cols_out[c, m, g * 4 + i] = value[at : at + R, :]

        def arrive_own(g=g):
            arrive(s, 3)
            hand_over(c, g, k).wait_recv()

        experts(c, k, g, store_own, arrive_own)
        return carry

    lax.fori_loop(0, 8, expert_step, 0)

    def last_rows(c, there):
        return sib.at[c, b0, pl.ds(pl.multiple_of(a0 * C + (there // 2) * R, R), R), 0:DN]

    def last_copies(c, act):
        def one(there):
            d = (there + nz - z) % nz
            act(z_copy(last_rows(c, there), zin2.at[d], there, last_ss, last_rs))

        toward(c, one)

    odd_first.start_far()
    column_copies(1, lambda copy: copy.start())
    even_first.finish()
    even_second.start()
    odd_first.pass_on()
    even_second.pass_on()
    even_second.finish()
    last_copies(0, lambda copy: copy.start())
    odd_first.finish()
    odd_second.start()
    odd_second.pass_on()
    odd_second.finish()
    last_copies(1, lambda copy: copy.start())
    column_totals()
    across = plane_copies()
    total = hid[:, DN:] + cols_sum[b0 * 4 + a0].astype(F32)
    for at, copy in enumerate(across):
        copy.wait_recv()
        total = total + cols_land[at + 1].astype(F32)
    out_ref[:, DN:] = total.astype(BF16)
    total = hid[:, 0:DN] + last_rows(z % 2, z)[...].astype(F32)
    for d in range(1, nz):
        z_copy(zin2.at[d], zin2.at[d], (z + d) % nz, last_ss, last_rs).wait_recv()
        total = total + zin2[d].astype(F32)
    out_ref[:, 0:DN] = total.astype(BF16)

    for scatter in (even_first, even_second, odd_first, odd_second):
        scatter.drain()
    for c in range(2):
        last_copies(c, lambda copy: copy.wait_send())
        column_copies(c, lambda copy: copy.wait_send())
        for g in range(4):
            hand_over(c, g, 1 - k).wait_send()
    for parity in range(2):
        toward(parity, lambda there: sum_copy(there).wait_send())

    for d in range(1, nz):
        z_copy(rows_at(z), rows_at(z), (z + d) % nz, row_ss, row_rs).wait_send()
    for copy in across:
        copy.wait_send()
    kv_gather.drain()
    even.drain()
    odd.drain()


def per_device(
    queries,
    key_rows,
    value_rows,
    residual,
    out_weight,
    norm_gain,
    gate_weight,
    up_weight,
    down_weight,
    routes,
    route_gates,
    block_picks,
):
    nz = lax.axis_size("exp")
    T, D = residual.shape
    R = T // nz
    C = T // 2
    tile = D // 8
    F = gate_weight.shape[2]
    wide = -(-2 * F // 128) * 128
    cols = queries.shape[1]
    nh = cols // HD
    vmem = pl.BlockSpec(memory_space=pltpu.VMEM)
    anywhere = pl.BlockSpec(memory_space=pl.ANY)
    dma = pltpu.SemaphoreType.DMA
    return pl.pallas_call(
        functools.partial(kernel, nz),
        out_shape=jax.ShapeDtypeStruct((R, D), BF16),
        in_specs=[vmem] * 6 + [pl.BlockSpec(memory_space=pltpu.SMEM)] + [anywhere] * 5,
        out_specs=vmem,
        scratch_shapes=[
            pltpu.VMEM((8, 4, 2 * T + INFO, cols), BF16),
            pltpu.VMEM((2, 8, 4 * C, D), BF16),
            pltpu.VMEM((2, 4, 4 * C, D), BF16),
            pltpu.VMEM((2, 2, 4 * C, D - tile), BF16),
            pltpu.VMEM((2, 2, 2 * C, D - tile), BF16),
            pltpu.VMEM((2, 2, C, D - tile), BF16),
            pltpu.VMEM((2, 2, C // 2, D - tile), BF16),
            pltpu.VMEM((T, D), BF16),
            pltpu.VMEM((nz, R, D), BF16),
            pltpu.VMEM((nz, R, D - tile), BF16),
            pltpu.VMEM((2, nz // 2, 16, R, tile), BF16),
            pltpu.VMEM((nz, 16, R, tile), BF16),
            pltpu.VMEM((16, R, tile), BF16),
            pltpu.VMEM((16, R, tile), BF16),
            pltpu.VMEM((T, D), F32),
            pltpu.VMEM((R, D), F32),
            pltpu.VMEM((INFO, T), F32),
            pltpu.VMEM((R, D), BF16),
            pltpu.VMEM(out_weight.shape, BF16),
            pltpu.VMEM((2 * wide, D), BF16),
            pltpu.VMEM((wide, D), BF16),
            pltpu.VMEM((4 * C, wide), BF16),
            pltpu.VMEM((T, 128), F32),
            pltpu.VMEM((2, 8, 4 * C, 128), F32),
            pltpu.VMEM((nh, T, 128), F32),
            pltpu.VMEM((nh, T, 128), F32),
            pltpu.VMEM((nh, T, HD), F32),
            dma((8,)),
            dma((36,)),
            dma((36,)),
            dma((72,)),
            dma((72,)),
            dma((8,)),
            dma((8,)),
            dma((24,)),
            dma((24,)),
            dma((nz,)),
            dma((nz,)),
            dma((nz,)),
            dma((nz,)),
            dma((nz,)),
            dma((nz,)),
            dma((nz,)),
            dma((nz,)),
            dma((16,)),
            dma((16,)),
            pltpu.SemaphoreType.REGULAR((3,)),
        ],
        compiler_params=pltpu.CompilerParams(
            collective_id=0, has_side_effects=True, vmem_limit_bytes=60 * 1024 * 1024
        ),
        cost_estimate=pl.CostEstimate(flops=2 * 10**10, bytes_accessed=10**7, transcendentals=10**6),
    )(
        queries,
        key_rows,
        value_rows,
        routes.T,
        route_gates.T,
        norm_gain.reshape(1, D),
        block_picks.T,
        residual,
        out_weight,
        jnp.swapaxes(gate_weight, 1, 2),
        jnp.swapaxes(up_weight, 1, 2),
        down_weight,
    )


def solution(mesh):
    placed = (
        P("seq", "exp"),
        P("seq", "exp"),
        P("seq", "exp"),
        P("seq", None),
        P("exp", None),
        P(),
        P("seq", None, "exp"),
        P("seq", None, "exp"),
        P("seq", "exp", None),
        P("seq", None),
        P("seq", None),
        P(),
    )
    return jax.shard_map(
        per_device, mesh=mesh, in_specs=placed, out_specs=P(("seq", "exp"), None), check_vma=False
    )
```
